32 devices in a mesh: group: 2 (over core), ctx: 16 (over z, y, x).
Axes of the slice: x: 2, y: 2, z: 4, core: 2. Of those that a mesh axis runs over, the one named last changes fastest.
Arguments:
- queries: bfloat16 [512, 4096], P(('group', 'ctx')), may hold values from -16 to 16
- key_states: bfloat16 [512, 4096], P(('group', 'ctx')), may hold values from -16 to 16
- value_states: bfloat16 [512, 4096], P(('group', 'ctx')), may hold values from -6 to 6
- gate_table: float32 [32, 4096], replicated, may hold values from 0.3 to 3
- noise_levels: int32 [2], replicated, may hold values from 0 to 31
- group_ids: int32 [2], replicated, may hold values from 0 to 1, each once
Outputs:
- handed: bfloat16 [512, 4096], P(('group', 'ctx'))
The draws below stay inside these ranges and needn't reach their ends.
Inputs may be any that keep to these rules, and one draw needn't show every extreme that they name: `group_ids`: each of 0 to 1 appears once.
All inputs are finite; a program needn't handle non-finite values.
Results may differ from the reference program's by a relative error of at most 0.007.
Values may be sent and summed in bfloat16 or wider, within the bound.
No kernel may reach another device: no remote copies, remote signals or barrier semaphores. Data moves between devices by JAX's collectives and lax.ppermute only.
A program may use at most 64 MiB of HBM per device.

```python
import math
import jax
import jax.numpy as jnp
from jax import lax

HEADS = 32
HEAD = 128
LEVELS = 32
GROUPS = 2
GROUP_TOK = 256
TOKENS = 512


def draw_queries(key, part):
    key = jax.random.fold_in(key, 11)
    base = jnp.clip(jax.random.normal(key, (TOKENS, HEADS * HEAD), jnp.float32), -5.0, 5.0)
    return base.astype(jnp.bfloat16)


def draw_key_states(key, part):
    key = jax.random.fold_in(key, 23)
    base = jnp.clip(jax.random.normal(key, (TOKENS, HEADS * HEAD), jnp.float32), -5.0, 5.0)
    return base.astype(jnp.bfloat16)


def steps_of(rng, extent, shards, least, high):
    level, own = 1.0, jax.random.fold_in(rng, 6)
    for axis_at, blocks in shards:
        steps = jnp.exp(jax.random.uniform(jax.random.fold_in(own, axis_at), (blocks,), jnp.float32, least / len(shards), high / len(shards)))
        level = level * jnp.repeat(steps, extent[axis_at] // blocks).reshape([-1 if axis == axis_at else 1 for axis in range(len(extent))])
    return level


def normal_values(own_key, extent, width, most, cuts=(), kind=jnp.bfloat16):
    factor_of = steps_of(own_key, extent, cuts, -0.22, 0.18) if cuts else 1.0
    result = jax.random.normal(own_key, extent, jnp.float32) * width * factor_of
    return jnp.minimum(jnp.maximum(result, -most), most).astype(kind)


def setup_inputs(seed: int = 0) -> dict:
    streams_of = jax.random.split(jax.random.key(seed), 7)
    queries = draw_queries(jax.random.fold_in(streams_of[6], 71), 0)
    key_states = draw_key_states(jax.random.fold_in(streams_of[6], 71), 0)
    value_states = normal_values(streams_of[2], (TOKENS, HEADS * HEAD), 1.0, 6.0, ((0, 32),))
    gate_table = jnp.clip(jnp.exp(jax.random.uniform(streams_of[3], (LEVELS, HEADS * HEAD), jnp.float32, math.log(0.3), math.log(3.0))), 0.3, 3.0)
    noise_levels = jax.random.randint(streams_of[4], (GROUPS,), 0, LEVELS).astype(jnp.int32)
    group_ids = jax.random.permutation(streams_of[5], GROUPS).astype(jnp.int32)
    return dict(queries=queries, key_states=key_states, value_states=value_states, gate_table=gate_table, noise_levels=noise_levels, group_ids=group_ids)


def reference(queries, key_states, value_states, gate_table, noise_levels, group_ids):
    score_scale = 1.0 / (HEAD ** 0.5)
    query_grid = queries.reshape(GROUPS, GROUP_TOK, HEADS, HEAD)
    key_grid = key_states.reshape(TOKENS, HEADS, HEAD)
    value_grid = value_states.reshape(TOKENS, HEADS, HEAD)
    key_ids = jnp.repeat(group_ids, GROUP_TOK)

    def one_head(index_pair):
        group_index, head_index = index_pair
        query_head = query_grid[group_index, :, head_index, :].astype(jnp.float32)
        key_head = key_grid[:, head_index, :].astype(jnp.float32)
        value_head = value_grid[:, head_index, :]
        scores = jnp.dot(query_head, key_head.T, precision=lax.Precision.HIGHEST) * score_scale
        allowed = (key_ids <= group_ids[group_index])[None, :]
        scores = jnp.where(allowed, scores, -1e30)
        peak = jnp.max(scores, axis=-1, keepdims=True)
        weights = jnp.where(allowed, jnp.exp(scores - peak), 0.0)
        total = jnp.sum(weights, axis=-1, keepdims=True)
        output = jnp.dot(weights.astype(jnp.bfloat16), value_head, preferred_element_type=jnp.float32) / total
        return output.astype(jnp.bfloat16)

    group_list = jnp.repeat(jnp.arange(GROUPS, dtype=jnp.int32), HEADS)
    head_list = jnp.tile(jnp.arange(HEADS, dtype=jnp.int32), GROUPS)
    attended = lax.map(one_head, (group_list, head_list))
    attended = attended.reshape(GROUPS, HEADS, GROUP_TOK, HEAD).transpose(0, 2, 1, 3)
    attended = attended.reshape(GROUPS, GROUP_TOK, HEADS * HEAD)
    gates = gate_table[noise_levels]
    done = (attended.astype(jnp.float32) * gates[:, None, :]).astype(jnp.bfloat16)
    return jnp.roll(done, 1, axis=0).reshape(TOKENS, HEADS * HEAD)
```

```python
import jax
import jax.numpy as jnp
from jax import lax
from jax.experimental import pallas as pl
from jax.experimental.pallas import tpu as pltpu
from jax.sharding import PartitionSpec as P

HEADS = 32
HEAD = 128
LOG2_E = 1.4426950408889634
TILE = 8
FIRST = 11
BITS = (3, 2, 1, 0)


def member_at(place):
    return FIRST ^ sum((place >> bit & 1) << to for bit, to in enumerate(BITS))


def place_of(member):
    return sum(((member ^ FIRST) >> to & 1) << bit for bit, to in enumerate(BITS))


def members_by_place(members):
    return [[member_at(place) for place in range(members)]]


def pack_kernel(
    levels_ref, ids_ref, gate_ref, query_ref, key_ref, value_ref,
    packed_ref, side_ref, levels, ids, gate_block, sems,
):
    width = gate_block.shape[1]
    place = place_of(lax.axis_index("ctx"))
    columns = pl.ds(pl.multiple_of(place * width, width), width)
    pairs = [(levels_ref, levels), (ids_ref, ids), (gate_ref.at[:, columns], gate_block)]
    for part, ref in enumerate((query_ref, key_ref, value_ref)):
        for tile in range(ref.shape[0]):
            pairs.append((ref.at[tile], packed_ref.at[:, part, :, tile]))
    fetches = [pltpu.make_async_copy(*pair, sems.at[i]) for i, pair in enumerate(pairs)]
    for fetch in fetches:
        fetch.start()
    for fetch in fetches[:3]:
        fetch.wait()
    own = lax.axis_index("group")
    other = 1 - own
    level_rows = lax.broadcasted_iota(jnp.int32, gate_block.shape, 0)
    gate = jnp.sum(jnp.where(level_rows == levels[other], gate_block[...], 0.0), axis=0, keepdims=True)
    mask = jnp.full((1, HEAD), jnp.where(ids[own] <= ids[other], 0.0, -1e30), jnp.float32)
    parts = [gate[:, at : at + HEAD] for at in range(0, width, HEAD)]
    side_ref[pl.ds(0, len(parts) + 1), :] = jnp.concatenate([*parts, mask], axis=0)
    for fetch in fetches[3:]:
        fetch.wait()


def attend_kernel(side_ref, own_ref, other_ref, out_ref):
    members, pair, rows, _ = out_ref.shape
    group_rows = members * rows
    factor = LOG2_E / HEAD**0.5

    def tokens(ref, part, head):
        return ref[:, pl.ds((part * pair + head) * rows, rows), :].reshape(group_rows, HEAD)

    def dot(a, b, contract):
        return lax.dot_general(a, b, ((contract[:1], contract[1:]), ((), ())), preferred_element_type=jnp.float32)

    ones = jnp.ones((group_rows, HEAD), jnp.bfloat16)
    mask = jnp.concatenate([side_ref[pair : pair + 1, :]] * (group_rows // HEAD), axis=1)
    for head in range(pair):
        queries = tokens(other_ref, 0, head)
        scores = [dot(queries, tokens(ref, 1, head), (1, 1)) for ref in (own_ref, other_ref)]
        scores[0] = scores[0] + mask
        peak = jnp.max(jnp.maximum(*scores), axis=1, keepdims=True)
        weights = [jnp.exp2((score - peak) * factor).astype(jnp.bfloat16) for score in scores]
        values = [jnp.concatenate([tokens(ref, 2, head), ones], axis=1) for ref in (own_ref, other_ref)]
        summed = sum(dot(weight, value, (1, 0)) for weight, value in zip(weights, values))
        attended = (summed[:, :HEAD] / summed[:, HEAD:]).astype(jnp.bfloat16)
        done = (attended.astype(jnp.float32) * side_ref[head : head + 1, :]).astype(jnp.bfloat16)
        out_ref[:, head] = done.reshape(members, rows, HEAD)


def unpack_kernel(heads_ref, out_ref, sems):
    copies = [
        pltpu.make_async_copy(heads_ref.at[:, :, tile], out_ref.at[tile], sems.at[tile])
        for tile in range(out_ref.shape[0])
    ]
    for copy in copies:
        copy.start()
    for copy in copies:
        copy.wait()


def in_vmem(array):
    return pltpu.with_memory_space_constraint(array, pltpu.VMEM)


def tiled(states, members):
    rows, columns = states.shape
    pair = columns // HEAD // members
    return states.reshape(rows // TILE, TILE, members, pair, HEAD).transpose(0, 2, 3, 1, 4)


def exchanged(chunks):
    members = members_by_place(chunks.shape[0])
    return lax.all_to_all(chunks, "ctx", split_axis=0, concat_axis=0, tiled=True, axis_index_groups=members)


def local(queries, key_states, value_states, gate_table, noise_levels, group_ids):
    rows = queries.shape[0]
    tiles = rows // TILE
    members = lax.axis_size("ctx")
    pair = HEADS // members
    whole = pl.BlockSpec(memory_space=pltpu.VMEM)
    hbm = pl.BlockSpec(memory_space=pltpu.HBM)
    states = (tiled(array, members) for array in (queries, key_states, value_states))
    sources = (noise_levels, group_ids, gate_table, *states)
    packed, side = pl.pallas_call(
        pack_kernel,
        out_shape=[
            pltpu.VMEM((members, 3, pair, tiles, TILE, HEAD), jnp.bfloat16),
            pltpu.VMEM((8, HEAD), jnp.float32),
        ],
        in_specs=[hbm] * len(sources),
        out_specs=[whole, whole],
        scratch_shapes=[
            pltpu.SMEM(noise_levels.shape, jnp.int32),
            pltpu.SMEM(group_ids.shape, jnp.int32),
            pltpu.VMEM((gate_table.shape[0], pair * HEAD), jnp.float32),
            pltpu.SemaphoreType.DMA((3 + 3 * tiles,)),
        ],
    )(*(pltpu.with_memory_space_constraint(source, pltpu.HBM) for source in sources))
    own = exchanged(packed.reshape(members, 3 * pair * rows, HEAD))
    other = lax.ppermute(own, "group", [(0, 1), (1, 0)])
    done = pl.pallas_call(
        attend_kernel,
        out_shape=pltpu.VMEM((members, pair, rows, HEAD), jnp.bfloat16),
        in_specs=[whole] * 3,
        out_specs=whole,
    )(in_vmem(side), in_vmem(own), in_vmem(other))
    returned = exchanged(done.reshape(members, pair * rows, HEAD))
    handed = pl.pallas_call(
        unpack_kernel,
        out_shape=pltpu.HBM((tiles, members, pair, TILE, HEAD), jnp.bfloat16),
        in_specs=[whole],
        out_specs=hbm,
        scratch_shapes=[pltpu.SemaphoreType.DMA((tiles,))],
    )(in_vmem(returned.reshape(members, pair, tiles, TILE, HEAD)))
    return handed.transpose(0, 3, 1, 2, 4).reshape(rows, HEADS * HEAD)


def shifted(block, axis, distance):
    devices = range(lax.axis_size(axis))
    route = [((i - distance) % len(devices), i) for i in devices]
    return lax.ppermute(block, axis, route)


def doubled(states):
    row_count = states.shape[0]
    shaped = states.reshape(row_count, HEADS, 1, HEAD)
    return jnp.broadcast_to(shaped, (row_count, HEADS, 2, HEAD)).reshape(row_count, 2 * HEADS, HEAD)


def attend(running, chosen, key_block, value_block, key_group, group_ids, own_id):
    peak, total, summed = running
    marked = key_group[:, None] == jnp.arange(group_ids.shape[0], dtype=jnp.int32)[None, :]
    key_ids = jnp.sum(jnp.where(marked, group_ids[None, :], 0), axis=1)
    allowed = (key_ids <= own_id)[None, None, :]
    scores = jnp.einsum("pqd,rpd->pqr", chosen, key_block, preferred_element_type=jnp.float32)
    scores = jnp.where(allowed, scores * (1.0 / HEAD**0.5), -1e30)
    new_peak = jnp.maximum(peak, jnp.max(scores, axis=-1))
    weights = jnp.where(allowed, jnp.exp(scores - new_peak[..., None]), 0.0)
    total = jnp.sum(weights, axis=-1)
    summed = jnp.einsum(
        "pqr,rpd->pqd",
        weights.astype(jnp.bfloat16),
        value_block,
        preferred_element_type=jnp.float32,
    )
    return (new_peak, total, summed)


def local_wide(queries, key_states, value_states, gate_table, noise_levels, group_ids):
    tok_count = queries.shape[0]
    ctx_count = lax.axis_size("ctx")
    group_count = lax.axis_size("group")
    slot_count = 2 * HEADS // ctx_count
    group_rows = tok_count * ctx_count
    half_rows = group_rows // 2
    section_marks = jnp.arange(group_count, dtype=jnp.int32) == lax.axis_index("group")
    own_id = jnp.sum(jnp.where(section_marks, group_ids, 0))
    own_level = jnp.sum(jnp.where(section_marks, noise_levels, 0))
    slot_index = lax.axis_index("ctx") * slot_count + jnp.arange(slot_count, dtype=jnp.int32)
    offsets = slot_index % 2 * half_rows

    def select(offset, block):
        return lax.dynamic_slice_in_dim(block, offset, half_rows, 0)

    initial = (
        jnp.full((slot_count, half_rows), -1e30, jnp.float32),
        jnp.zeros((slot_count, half_rows), jnp.float32),
        jnp.zeros((slot_count, half_rows, HEAD), jnp.float32),
    )
    query_heads, key_heads, value_heads = (
        lax.all_to_all(doubled(queries), "ctx", split_axis=1, concat_axis=0, tiled=True),
        lax.all_to_all(doubled(key_states), "ctx", split_axis=1, concat_axis=0, tiled=True),
        lax.all_to_all(doubled(value_states), "ctx", split_axis=1, concat_axis=0, tiled=True),
    )
    chosen = jax.vmap(select, in_axes=(0, 1))(offsets, query_heads)
    key_piece = lax.all_gather(key_heads, "group", axis=0, tiled=True)
    value_piece = lax.all_gather(value_heads, "group", axis=0, tiled=True)
    key_group = jnp.arange(key_piece.shape[0], dtype=jnp.int32) // group_rows
    running = attend(initial, chosen, key_piece, value_piece, key_group, group_ids, own_id)
    peak, total, summed = running
    attended = (summed / total[..., None]).astype(jnp.bfloat16)

    def place(offset, block):
        return lax.dynamic_update_slice_in_dim(
            jnp.zeros((group_rows, HEAD), jnp.bfloat16), block, offset, 0
        )

    spread = jax.vmap(place, out_axes=1)(offsets, attended)
    returned = lax.all_to_all(spread, "ctx", split_axis=0, concat_axis=1, tiled=True)
    paired = returned.reshape(tok_count, HEADS, 2, HEAD)
    merged = (paired[:, :, 0] + paired[:, :, 1]).reshape(tok_count, HEADS * HEAD)
    level_marks = jnp.arange(gate_table.shape[0], dtype=jnp.int32)[:, None] == own_level
    gate_row = jnp.sum(jnp.where(level_marks, gate_table, 0.0), axis=0)
    done = (merged.astype(jnp.float32) * gate_row[None, :]).astype(jnp.bfloat16)
    return shifted(done, "group", 1)


def solution(mesh):
    in_pairs = mesh.shape["group"] == 2 and 2 * mesh.shape["ctx"] == HEADS == 2 << len(BITS)
    tokens = P(("group", "ctx"), None)
    return jax.shard_map(
        local if in_pairs else local_wide,
        mesh=mesh,
        in_specs=(tokens, tokens, tokens, P(), P(), P()),
        out_specs=tokens,
        check_vma=False,
    )
```

```python
import functools

import jax
import jax.numpy as jnp
from jax import lax
from jax.experimental import pallas as pl
from jax.experimental.pallas import tpu as pltpu
from jax.sharding import PartitionSpec as P

HEADS = 32
HEAD = 128
LOG2_E = 1.4426950408889634
TILE = 8
FIRST = 11
SWAPPED = (0,)


def teams(members):
    order = [place ^ FIRST for place in range(members)]
    return [[(team ^ (member in SWAPPED)) * members + member for member in order] for team in range(2)]


def own_team():
    team = lax.axis_index("group")
    for member in SWAPPED:
        team = jnp.where(lax.axis_index("ctx") == member, 1 - team, team)
    return team


def pack_kernel(
    levels_ref, ids_ref, gate_ref, query_ref, key_ref, value_ref,
    packed_ref, side_ref, levels, ids, gate_block, sems,
):
    width = gate_block.shape[1]
    place = lax.axis_index("ctx") ^ FIRST
    columns = pl.ds(pl.multiple_of(place * width, width), width)
    pairs = [(levels_ref, levels), (ids_ref, ids), (gate_ref.at[:, columns], gate_block)]
    for part, ref in enumerate((query_ref, key_ref, value_ref)):
        for tile in range(ref.shape[0]):
            pairs.append((ref.at[tile], packed_ref.at[:, part, :, tile]))
    fetches = [pltpu.make_async_copy(*pair, sems.at[i]) for i, pair in enumerate(pairs)]
    for fetch in fetches:
        fetch.start()
    for fetch in fetches[:3]:
        fetch.wait()
    own = own_team()
    other = 1 - own
    level_rows = lax.broadcasted_iota(jnp.int32, gate_block.shape, 0)

    def gate(group):
        return jnp.sum(jnp.where(level_rows == levels[group], gate_block[...], 0.0), axis=0, keepdims=True)

    keys = side_ref.shape[1]
    key_place = lax.broadcasted_iota(jnp.int32, (1, keys), 1) // (keys // packed_ref.shape[0])
    key_swapped = functools.reduce(jnp.logical_or, [key_place == member ^ FIRST for member in SWAPPED])
    straight = jnp.where(ids[own] <= ids[other], 0.0, -1e30)
    crossed = jnp.where(ids[other] <= ids[own], 0.0, -1e30)
    masks = [
        jnp.where(key_swapped, 0.0, straight),
        jnp.where(key_swapped, straight, 0.0),
        jnp.where(key_swapped, crossed, 0.0),
        jnp.where(key_swapped, 0.0, crossed),
    ]
    side_ref[pl.ds(0, 6), :] = jnp.concatenate([gate(other), gate(own), *masks], axis=0)
    for fetch in fetches[3:]:
        fetch.wait()


def attend_kernel(side_ref, own_ref, other_ref, out_ref):
    members, pair, rows, _ = out_ref.shape
    group_rows = members * rows
    factor = LOG2_E / HEAD**0.5
    swapped = [place ^ FIRST in SWAPPED for place in range(members)]
    cuts = [0, *(place for place in range(1, members) if swapped[place] != swapped[place - 1]), members]
    runs = [(slice(start * rows, stop * rows), swapped[start]) for start, stop in zip(cuts, cuts[1:])]

    def tokens(ref, part, head):
        return ref[:, pl.ds((part * pair + head) * rows, rows), :].reshape(group_rows, HEAD)

    def dot(a, b, contract):
        return lax.dot_general(a, b, ((contract[:1], contract[1:]), ((), ())), preferred_element_type=jnp.float32)

    def masked(score, side):
        masks = [side_ref[2 + 2 * kind + side : 3 + 2 * kind + side, :] for kind in range(2)]
        return jnp.concatenate([score[run] + masks[kind] for run, kind in runs], axis=0)

    ones = jnp.ones((group_rows, HEAD), jnp.bfloat16)
    for head in range(pair):
        queries = tokens(other_ref, 0, head)
        refs = (own_ref, other_ref)
        scores = [masked(dot(queries, tokens(ref, 1, head), (1, 1)), side) for side, ref in enumerate(refs)]
        peak = jnp.max(jnp.maximum(*scores), axis=1, keepdims=True)
        weights = [jnp.exp2((score - peak) * factor).astype(jnp.bfloat16) for score in scores]
        values = [jnp.concatenate([tokens(ref, 2, head), ones], axis=1) for ref in refs]
        summed = sum(dot(weight, value, (1, 0)) for weight, value in zip(weights, values))
        attended = (summed[:, :HEAD] / summed[:, HEAD:]).astype(jnp.bfloat16).astype(jnp.float32)
        gates = [side_ref[kind : kind + 1, head * HEAD : (head + 1) * HEAD] for kind in range(2)]
        done = jnp.concatenate([attended[run] * gates[kind] for run, kind in runs], axis=0).astype(jnp.bfloat16)
        out_ref[:, head] = done.reshape(members, rows, HEAD)


def unpack_kernel(heads_ref, out_ref, sems):
    copies = [
        pltpu.make_async_copy(heads_ref.at[:, :, tile], out_ref.at[tile], sems.at[tile])
        for tile in range(out_ref.shape[0])
    ]
    for copy in copies:
        copy.start()
    for copy in copies:
        copy.wait()


def in_vmem(array):
    return pltpu.with_memory_space_constraint(array, pltpu.VMEM)


def tiled(states, members):
    rows, columns = states.shape
    pair = columns // HEAD // members
    return states.reshape(rows // TILE, TILE, members, pair, HEAD).transpose(0, 2, 3, 1, 4)


def exchanged(chunks):
    groups = teams(chunks.shape[0])
    return lax.all_to_all(chunks, ("group", "ctx"), split_axis=0, concat_axis=0, tiled=True, axis_index_groups=groups)


def local(queries, key_states, value_states, gate_table, noise_levels, group_ids):
    rows = queries.shape[0]
    tiles = rows // TILE
    members = lax.axis_size("ctx")
    pair = HEADS // members
    whole = pl.BlockSpec(memory_space=pltpu.VMEM)
    hbm = pl.BlockSpec(memory_space=pltpu.HBM)
    states = (tiled(array, members) for array in (queries, key_states, value_states))
    sources = (noise_levels, group_ids, gate_table, *states)
    packed, side = pl.pallas_call(
        pack_kernel,
        out_shape=[
            pltpu.VMEM((members, 3, pair, tiles, TILE, HEAD), jnp.bfloat16),
            pltpu.VMEM((8, members * rows), jnp.float32),
        ],
        in_specs=[hbm] * len(sources),
        out_specs=[whole, whole],
        scratch_shapes=[
            pltpu.SMEM(noise_levels.shape, jnp.int32),
            pltpu.SMEM(group_ids.shape, jnp.int32),
            pltpu.VMEM((gate_table.shape[0], pair * HEAD), jnp.float32),
            pltpu.SemaphoreType.DMA((3 + 3 * tiles,)),
        ],
    )(*(pltpu.with_memory_space_constraint(source, pltpu.HBM) for source in sources))
    own = exchanged(packed.reshape(members, 3 * pair * rows, HEAD))
    other = lax.ppermute(own, "group", [(0, 1), (1, 0)])
    done = pl.pallas_call(
        attend_kernel,
        out_shape=pltpu.VMEM((members, pair, rows, HEAD), jnp.bfloat16),
        in_specs=[whole] * 3,
        out_specs=whole,
    )(in_vmem(side), in_vmem(own), in_vmem(other))
    returned = exchanged(done.reshape(members, pair * rows, HEAD))
    handed = pl.pallas_call(
        unpack_kernel,
        out_shape=pltpu.HBM((tiles, members, pair, TILE, HEAD), jnp.bfloat16),
        in_specs=[whole],
        out_specs=hbm,
        scratch_shapes=[pltpu.SemaphoreType.DMA((tiles,))],
    )(in_vmem(returned.reshape(members, pair, tiles, TILE, HEAD)))
    return handed.transpose(0, 3, 1, 2, 4).reshape(rows, HEADS * HEAD)


def shifted(block, axis, distance):
    devices = range(lax.axis_size(axis))
    route = [((i - distance) % len(devices), i) for i in devices]
    return lax.ppermute(block, axis, route)


def doubled(states):
    row_count = states.shape[0]
    shaped = states.reshape(row_count, HEADS, 1, HEAD)
    return jnp.broadcast_to(shaped, (row_count, HEADS, 2, HEAD)).reshape(row_count, 2 * HEADS, HEAD)


def attend(running, chosen, key_block, value_block, key_group, group_ids, own_id):
    peak, total, summed = running
    marked = key_group[:, None] == jnp.arange(group_ids.shape[0], dtype=jnp.int32)[None, :]
    key_ids = jnp.sum(jnp.where(marked, group_ids[None, :], 0), axis=1)
    allowed = (key_ids <= own_id)[None, None, :]
    scores = jnp.einsum("pqd,rpd->pqr", chosen, key_block, preferred_element_type=jnp.float32)
    scores = jnp.where(allowed, scores * (1.0 / HEAD**0.5), -1e30)
    new_peak = jnp.maximum(peak, jnp.max(scores, axis=-1))
    weights = jnp.where(allowed, jnp.exp(scores - new_peak[..., None]), 0.0)
    total = jnp.sum(weights, axis=-1)
    summed = jnp.einsum(
        "pqr,rpd->pqd",
        weights.astype(jnp.bfloat16),
        value_block,
        preferred_element_type=jnp.float32,
    )
    return (new_peak, total, summed)


def local_wide(queries, key_states, value_states, gate_table, noise_levels, group_ids):
    tok_count = queries.shape[0]
    ctx_count = lax.axis_size("ctx")
    group_count = lax.axis_size("group")
    slot_count = 2 * HEADS // ctx_count
    group_rows = tok_count * ctx_count
    half_rows = group_rows // 2
    section_marks = jnp.arange(group_count, dtype=jnp.int32) == lax.axis_index("group")
    own_id = jnp.sum(jnp.where(section_marks, group_ids, 0))
    own_level = jnp.sum(jnp.where(section_marks, noise_levels, 0))
    slot_index = lax.axis_index("ctx") * slot_count + jnp.arange(slot_count, dtype=jnp.int32)
    offsets = slot_index % 2 * half_rows

    def select(offset, block):
        return lax.dynamic_slice_in_dim(block, offset, half_rows, 0)

    initial = (
        jnp.full((slot_count, half_rows), -1e30, jnp.float32),
        jnp.zeros((slot_count, half_rows), jnp.float32),
        jnp.zeros((slot_count, half_rows, HEAD), jnp.float32),
    )
    query_heads, key_heads, value_heads = (
        lax.all_to_all(doubled(queries), "ctx", split_axis=1, concat_axis=0, tiled=True),
        lax.all_to_all(doubled(key_states), "ctx", split_axis=1, concat_axis=0, tiled=True),
        lax.all_to_all(doubled(value_states), "ctx", split_axis=1, concat_axis=0, tiled=True),
    )
    chosen = jax.vmap(select, in_axes=(0, 1))(offsets, query_heads)
    key_piece = lax.all_gather(key_heads, "group", axis=0, tiled=True)
    value_piece = lax.all_gather(value_heads, "group", axis=0, tiled=True)
    key_group = jnp.arange(key_piece.shape[0], dtype=jnp.int32) // group_rows
    running = attend(initial, chosen, key_piece, value_piece, key_group, group_ids, own_id)
    peak, total, summed = running
    attended = (summed / total[..., None]).astype(jnp.bfloat16)

    def place(offset, block):
        return lax.dynamic_update_slice_in_dim(
            jnp.zeros((group_rows, HEAD), jnp.bfloat16), block, offset, 0
        )

    spread = jax.vmap(place, out_axes=1)(offsets, attended)
    returned = lax.all_to_all(spread, "ctx", split_axis=0, concat_axis=1, tiled=True)
    paired = returned.reshape(tok_count, HEADS, 2, HEAD)
    merged = (paired[:, :, 0] + paired[:, :, 1]).reshape(tok_count, HEADS * HEAD)
    level_marks = jnp.arange(gate_table.shape[0], dtype=jnp.int32)[:, None] == own_level
    gate_row = jnp.sum(jnp.where(level_marks, gate_table, 0.0), axis=0)
    done = (merged.astype(jnp.float32) * gate_row[None, :]).astype(jnp.bfloat16)
    return shifted(done, "group", 1)


def solution(mesh):
    in_pairs = mesh.shape["group"] == 2 and 2 * mesh.shape["ctx"] == HEADS
    tokens = P(("group", "ctx"), None)
    return jax.shard_map(
        local if in_pairs else local_wide,
        mesh=mesh,
        in_specs=(tokens, tokens, tokens, P(), P(), P()),
        out_specs=tokens,
        check_vma=False,
    )
```

```python
import functools

import jax
import jax.numpy as jnp
from jax import lax
from jax.experimental import pallas as pl
from jax.experimental.pallas import tpu as pltpu
from jax.sharding import PartitionSpec as P

HEADS = 32
HEAD = 128
LOG2_E = 1.4426950408889634
TILE = 8
FIRST = 11
SWAPPED = (0,)
STATES_BITS = (3, 2, 1, 0)
DONE_BITS = (0, 1, 2, 3)


def member_at(place, bits):
    return FIRST ^ sum((place >> bit & 1) << to for bit, to in enumerate(bits))


def place_of(member, bits):
    return sum(((member ^ FIRST) >> to & 1) << bit for bit, to in enumerate(bits))


def done_place(place):
    return place_of(member_at(place, STATES_BITS), DONE_BITS)


def teams(members, bits):
    order = [member_at(place, bits) for place in range(members)]
    return [[(team ^ (member in SWAPPED)) * members + member for member in order] for team in range(2)]


def own_team():
    team = lax.axis_index("group")
    for member in SWAPPED:
        team = jnp.where(lax.axis_index("ctx") == member, 1 - team, team)
    return team


def pack_kernel(
    levels_ref, ids_ref, gate_ref, query_ref, key_ref, value_ref,
    packed_ref, side_ref, levels, ids, gate_block, sems,
):
    width = gate_block.shape[1]
    place = place_of(lax.axis_index("ctx"), STATES_BITS)
    columns = pl.ds(pl.multiple_of(place * width, width), width)
    pairs = [(levels_ref, levels), (ids_ref, ids), (gate_ref.at[:, columns], gate_block)]
    for part, ref in enumerate((query_ref, key_ref, value_ref)):
        for tile in range(ref.shape[0]):
            pairs.append((ref.at[tile], packed_ref.at[:, part, :, tile]))
    fetches = [pltpu.make_async_copy(*pair, sems.at[i]) for i, pair in enumerate(pairs)]
    for fetch in fetches:
        fetch.start()
    for fetch in fetches[:3]:
        fetch.wait()
    own = own_team()
    other = 1 - own
    level_rows = lax.broadcasted_iota(jnp.int32, gate_block.shape, 0)

    def gate(group):
        return jnp.sum(jnp.where(level_rows == levels[group], gate_block[...], 0.0), axis=0, keepdims=True)

    keys = side_ref.shape[1]
    key_place = lax.broadcasted_iota(jnp.int32, (1, keys), 1) // (keys // packed_ref.shape[0])
    key_swapped = functools.reduce(jnp.logical_or, [key_place == place_of(member, STATES_BITS) for member in SWAPPED])
    straight = jnp.where(ids[own] <= ids[other], 0.0, -1e30)
    crossed = jnp.where(ids[other] <= ids[own], 0.0, -1e30)
    masks = [
        jnp.where(key_swapped, 0.0, straight),
        jnp.where(key_swapped, straight, 0.0),
        jnp.where(key_swapped, crossed, 0.0),
        jnp.where(key_swapped, 0.0, crossed),
    ]
    side_ref[pl.ds(0, 6), :] = jnp.concatenate([gate(other), gate(own), *masks], axis=0)
    for fetch in fetches[3:]:
        fetch.wait()


def attend_kernel(side_ref, own_ref, other_ref, out_ref):
    members, pair, rows, _ = out_ref.shape
    group_rows = members * rows
    factor = LOG2_E / HEAD**0.5
    swapped = [member_at(place, STATES_BITS) in SWAPPED for place in range(members)]
    cuts = [0, *(place for place in range(1, members) if swapped[place] != swapped[place - 1]), members]
    runs = [(slice(start * rows, stop * rows), swapped[start]) for start, stop in zip(cuts, cuts[1:])]

    def tokens(ref, part, head):
        return ref[:, pl.ds((part * pair + head) * rows, rows), :].reshape(group_rows, HEAD)

    def dot(a, b, contract):
        return lax.dot_general(a, b, ((contract[:1], contract[1:]), ((), ())), preferred_element_type=jnp.float32)

    def masked(score, side):
        masks = [side_ref[2 + 2 * kind + side : 3 + 2 * kind + side, :] for kind in range(2)]
        return jnp.concatenate([score[run] + masks[kind] for run, kind in runs], axis=0)

    ones = jnp.ones((group_rows, HEAD), jnp.bfloat16)
    for head in range(pair):
        queries = tokens(other_ref, 0, head)
        refs = (own_ref, other_ref)
        scores = [masked(dot(queries, tokens(ref, 1, head), (1, 1)), side) for side, ref in enumerate(refs)]
        peak = jnp.max(jnp.maximum(*scores), axis=1, keepdims=True)
        weights = [jnp.exp2((score - peak) * factor).astype(jnp.bfloat16) for score in scores]
        values = [jnp.concatenate([tokens(ref, 2, head), ones], axis=1) for ref in refs]
        summed = sum(dot(weight, value, (1, 0)) for weight, value in zip(weights, values))
        attended = (summed[:, :HEAD] / summed[:, HEAD:]).astype(jnp.bfloat16).astype(jnp.float32)
        gates = [side_ref[kind : kind + 1, head * HEAD : (head + 1) * HEAD] for kind in range(2)]
        done = jnp.concatenate([attended[run] * gates[kind] for run, kind in runs], axis=0).astype(jnp.bfloat16)
        for place in range(members):
            out_ref[done_place(place), head] = done[place * rows : (place + 1) * rows]


def unpack_kernel(heads_ref, out_ref):
    members, pair, rows, _ = heads_ref.shape
    for place in range(members):
        for head in range(pair):
            out_ref[:, pl.ds((place * pair + head) * HEAD, HEAD)] = heads_ref[done_place(place), head]


def in_vmem(array):
    return pltpu.with_memory_space_constraint(array, pltpu.VMEM)


def tiled(states, members):
    rows, columns = states.shape
    pair = columns // HEAD // members
    return states.reshape(rows // TILE, TILE, members, pair, HEAD).transpose(0, 2, 3, 1, 4)


def exchanged(chunks, bits):
    groups = teams(chunks.shape[0], bits)
    return lax.all_to_all(chunks, ("group", "ctx"), split_axis=0, concat_axis=0, tiled=True, axis_index_groups=groups)


def local(queries, key_states, value_states, gate_table, noise_levels, group_ids):
    rows = queries.shape[0]
    tiles = rows // TILE
    members = lax.axis_size("ctx")
    pair = HEADS // members
    whole = pl.BlockSpec(memory_space=pltpu.VMEM)
    hbm = pl.BlockSpec(memory_space=pltpu.HBM)
    states = (tiled(array, members) for array in (queries, key_states, value_states))
    sources = (noise_levels, group_ids, gate_table, *states)
    packed, side = pl.pallas_call(
        pack_kernel,
        out_shape=[
            pltpu.VMEM((members, 3, pair, tiles, TILE, HEAD), jnp.bfloat16),
            pltpu.VMEM((8, members * rows), jnp.float32),
        ],
        in_specs=[hbm] * len(sources),
        out_specs=[whole, whole],
        scratch_shapes=[
            pltpu.SMEM(noise_levels.shape, jnp.int32),
            pltpu.SMEM(group_ids.shape, jnp.int32),
            pltpu.VMEM((gate_table.shape[0], pair * HEAD), jnp.float32),
            pltpu.SemaphoreType.DMA((3 + 3 * tiles,)),
        ],
    )(*(pltpu.with_memory_space_constraint(source, pltpu.HBM) for source in sources))
    own = exchanged(packed.reshape(members, 3 * pair * rows, HEAD), STATES_BITS)
    other = lax.ppermute(own, "group", [(0, 1), (1, 0)])
    done = pl.pallas_call(
        attend_kernel,
        out_shape=pltpu.VMEM((members, pair, rows, HEAD), jnp.bfloat16),
        in_specs=[whole] * 3,
        out_specs=whole,
    )(in_vmem(side), in_vmem(own), in_vmem(other))
    returned = exchanged(done.reshape(members, pair * rows, HEAD), DONE_BITS)
    return pl.pallas_call(
        unpack_kernel,
        out_shape=jax.ShapeDtypeStruct((rows, HEADS * HEAD), jnp.bfloat16),
        in_specs=[whole],
        out_specs=whole,
    )(in_vmem(returned.reshape(members, pair, rows, HEAD)))


def shifted(block, axis, distance):
    devices = range(lax.axis_size(axis))
    route = [((i - distance) % len(devices), i) for i in devices]
    return lax.ppermute(block, axis, route)


def doubled(states):
    row_count = states.shape[0]
    shaped = states.reshape(row_count, HEADS, 1, HEAD)
    return jnp.broadcast_to(shaped, (row_count, HEADS, 2, HEAD)).reshape(row_count, 2 * HEADS, HEAD)


def attend(running, chosen, key_block, value_block, key_group, group_ids, own_id):
    peak, total, summed = running
    marked = key_group[:, None] == jnp.arange(group_ids.shape[0], dtype=jnp.int32)[None, :]
    key_ids = jnp.sum(jnp.where(marked, group_ids[None, :], 0), axis=1)
    allowed = (key_ids <= own_id)[None, None, :]
    scores = jnp.einsum("pqd,rpd->pqr", chosen, key_block, preferred_element_type=jnp.float32)
    scores = jnp.where(allowed, scores * (1.0 / HEAD**0.5), -1e30)
    new_peak = jnp.maximum(peak, jnp.max(scores, axis=-1))
    weights = jnp.where(allowed, jnp.exp(scores - new_peak[..., None]), 0.0)
    total = jnp.sum(weights, axis=-1)
    summed = jnp.einsum(
        "pqr,rpd->pqd",
        weights.astype(jnp.bfloat16),
        value_block,
        preferred_element_type=jnp.float32,
    )
    return (new_peak, total, summed)


def local_wide(queries, key_states, value_states, gate_table, noise_levels, group_ids):
    tok_count = queries.shape[0]
    ctx_count = lax.axis_size("ctx")
    group_count = lax.axis_size("group")
    slot_count = 2 * HEADS // ctx_count
    group_rows = tok_count * ctx_count
    half_rows = group_rows // 2
    section_marks = jnp.arange(group_count, dtype=jnp.int32) == lax.axis_index("group")
    own_id = jnp.sum(jnp.where(section_marks, group_ids, 0))
    own_level = jnp.sum(jnp.where(section_marks, noise_levels, 0))
    slot_index = lax.axis_index("ctx") * slot_count + jnp.arange(slot_count, dtype=jnp.int32)
    offsets = slot_index % 2 * half_rows

    def select(offset, block):
        return lax.dynamic_slice_in_dim(block, offset, half_rows, 0)

    initial = (
        jnp.full((slot_count, half_rows), -1e30, jnp.float32),
        jnp.zeros((slot_count, half_rows), jnp.float32),
        jnp.zeros((slot_count, half_rows, HEAD), jnp.float32),
    )
    query_heads, key_heads, value_heads = (
        lax.all_to_all(doubled(queries), "ctx", split_axis=1, concat_axis=0, tiled=True),
        lax.all_to_all(doubled(key_states), "ctx", split_axis=1, concat_axis=0, tiled=True),
        lax.all_to_all(doubled(value_states), "ctx", split_axis=1, concat_axis=0, tiled=True),
    )
    chosen = jax.vmap(select, in_axes=(0, 1))(offsets, query_heads)
    key_piece = lax.all_gather(key_heads, "group", axis=0, tiled=True)
    value_piece = lax.all_gather(value_heads, "group", axis=0, tiled=True)
    key_group = jnp.arange(key_piece.shape[0], dtype=jnp.int32) // group_rows
    running = attend(initial, chosen, key_piece, value_piece, key_group, group_ids, own_id)
    peak, total, summed = running
    attended = (summed / total[..., None]).astype(jnp.bfloat16)

    def place(offset, block):
        return lax.dynamic_update_slice_in_dim(
            jnp.zeros((group_rows, HEAD), jnp.bfloat16), block, offset, 0
        )

    spread = jax.vmap(place, out_axes=1)(offsets, attended)
    returned = lax.all_to_all(spread, "ctx", split_axis=0, concat_axis=1, tiled=True)
    paired = returned.reshape(tok_count, HEADS, 2, HEAD)
    merged = (paired[:, :, 0] + paired[:, :, 1]).reshape(tok_count, HEADS * HEAD)
    level_marks = jnp.arange(gate_table.shape[0], dtype=jnp.int32)[:, None] == own_level
    gate_row = jnp.sum(jnp.where(level_marks, gate_table, 0.0), axis=0)
    done = (merged.astype(jnp.float32) * gate_row[None, :]).astype(jnp.bfloat16)
    return shifted(done, "group", 1)


def solution(mesh):
    in_pairs = mesh.shape["group"] == 2 and 2 * mesh.shape["ctx"] == HEADS == 2 << len(STATES_BITS)
    tokens = P(("group", "ctx"), None)
    return jax.shard_map(
        local if in_pairs else local_wide,
        mesh=mesh,
        in_specs=(tokens, tokens, tokens, P(), P(), P()),
        out_specs=tokens,
        check_vma=False,
    )
```

```python
import functools

import jax
import jax.numpy as jnp
from jax import lax
from jax.experimental import pallas as pl
from jax.experimental.pallas import tpu as pltpu
from jax.sharding import PartitionSpec as P

HEADS = 32
HEAD = 128
LOG2_E = 1.4426950408889634
TILE = 8
FIRST = 11
STEP = -1
SWAPPED = (0,)


def member_at(place, members):
    return (FIRST + STEP * place) % members


def place_of(member, members):
    return (member - FIRST) * STEP % members


def teams(members):
    order = [member_at(place, members) for place in range(members)]
    return [[(team ^ (member in SWAPPED)) * members + member for member in order] for team in range(2)]


def own_team():
    team = lax.axis_index("group")
    for member in SWAPPED:
        team = jnp.where(lax.axis_index("ctx") == member, 1 - team, team)
    return team


def pack_kernel(
    levels_ref, ids_ref, gate_ref, query_ref, key_ref, value_ref,
    packed_ref, side_ref, levels, ids, gate_block, sems,
):
    width = gate_block.shape[1]
    members = packed_ref.shape[0]
    place = (FIRST + members - lax.axis_index("ctx")) % members
    columns = pl.ds(pl.multiple_of(place * width, width), width)
    pairs = [(levels_ref, levels), (ids_ref, ids), (gate_ref.at[:, columns], gate_block)]
    for part, ref in enumerate((query_ref, key_ref, value_ref)):
        for tile in range(ref.shape[0]):
            pairs.append((ref.at[tile], packed_ref.at[:, part, :, tile]))
    fetches = [pltpu.make_async_copy(*pair, sems.at[i]) for i, pair in enumerate(pairs)]
    for fetch in fetches:
        fetch.start()
    for fetch in fetches[:3]:
        fetch.wait()
    own = own_team()
    other = 1 - own
    level_rows = lax.broadcasted_iota(jnp.int32, gate_block.shape, 0)

    def gate(group):
        return jnp.sum(jnp.where(level_rows == levels[group], gate_block[...], 0.0), axis=0, keepdims=True)

    keys = side_ref.shape[1]
    key_place = lax.broadcasted_iota(jnp.int32, (1, keys), 1) // (keys // packed_ref.shape[0])
    key_swapped = functools.reduce(jnp.logical_or, [key_place == place_of(member, members) for member in SWAPPED])
    straight = jnp.where(ids[own] <= ids[other], 0.0, -1e30)
    crossed = jnp.where(ids[other] <= ids[own], 0.0, -1e30)
    masks = [
        jnp.where(key_swapped, 0.0, straight),
        jnp.where(key_swapped, straight, 0.0),
        jnp.where(key_swapped, crossed, 0.0),
        jnp.where(key_swapped, 0.0, crossed),
    ]
    side_ref[pl.ds(0, 6), :] = jnp.concatenate([gate(other), gate(own), *masks], axis=0)
    for fetch in fetches[3:]:
        fetch.wait()


def attend_kernel(side_ref, own_ref, other_ref, out_ref):
    members, pair, rows, _ = out_ref.shape
    group_rows = members * rows
    factor = LOG2_E / HEAD**0.5
    swapped = [member_at(place, members) in SWAPPED for place in range(members)]
    cuts = [0, *(place for place in range(1, members) if swapped[place] != swapped[place - 1]), members]
    runs = [(slice(start * rows, stop * rows), swapped[start]) for start, stop in zip(cuts, cuts[1:])]

    def tokens(ref, part, head):
        return ref[:, pl.ds((part * pair + head) * rows, rows), :].reshape(group_rows, HEAD)

    def dot(a, b, contract):
        return lax.dot_general(a, b, ((contract[:1], contract[1:]), ((), ())), preferred_element_type=jnp.float32)

    def masked(score, side):
        masks = [side_ref[2 + 2 * kind + side : 3 + 2 * kind + side, :] for kind in range(2)]
        return jnp.concatenate([score[run] + masks[kind] for run, kind in runs], axis=0)

    ones = jnp.ones((group_rows, HEAD), jnp.bfloat16)
    for head in range(pair):
        queries = tokens(other_ref, 0, head)
        refs = (own_ref, other_ref)
        scores = [masked(dot(queries, tokens(ref, 1, head), (1, 1)), side) for side, ref in enumerate(refs)]
        peak = jnp.max(jnp.maximum(*scores), axis=1, keepdims=True)
        weights = [jnp.exp2((score - peak) * factor).astype(jnp.bfloat16) for score in scores]
        values = [jnp.concatenate([tokens(ref, 2, head), ones], axis=1) for ref in refs]
        summed = sum(dot(weight, value, (1, 0)) for weight, value in zip(weights, values))
        attended = (summed[:, :HEAD] / summed[:, HEAD:]).astype(jnp.bfloat16).astype(jnp.float32)
        gates = [side_ref[kind : kind + 1, head * HEAD : (head + 1) * HEAD] for kind in range(2)]
        done = jnp.concatenate([attended[run] * gates[kind] for run, kind in runs], axis=0).astype(jnp.bfloat16)
        out_ref[:, head] = done.reshape(members, rows, HEAD)


def unpack_kernel(heads_ref, out_ref, sems):
    copies = [
        pltpu.make_async_copy(heads_ref.at[:, :, tile], out_ref.at[tile], sems.at[tile])
        for tile in range(out_ref.shape[0])
    ]
    for copy in copies:
        copy.start()
    for copy in copies:
        copy.wait()


def in_vmem(array):
    return pltpu.with_memory_space_constraint(array, pltpu.VMEM)


def tiled(states, members):
    rows, columns = states.shape
    pair = columns // HEAD // members
    return states.reshape(rows // TILE, TILE, members, pair, HEAD).transpose(0, 2, 3, 1, 4)


def exchanged(chunks):
    groups = teams(chunks.shape[0])
    return lax.all_to_all(chunks, ("group", "ctx"), split_axis=0, concat_axis=0, tiled=True, axis_index_groups=groups)


def local(queries, key_states, value_states, gate_table, noise_levels, group_ids):
    rows = queries.shape[0]
    tiles = rows // TILE
    members = lax.axis_size("ctx")
    pair = HEADS // members
    whole = pl.BlockSpec(memory_space=pltpu.VMEM)
    hbm = pl.BlockSpec(memory_space=pltpu.HBM)
    states = (tiled(array, members) for array in (queries, key_states, value_states))
    sources = (noise_levels, group_ids, gate_table, *states)
    packed, side = pl.pallas_call(
        pack_kernel,
        out_shape=[
            pltpu.VMEM((members, 3, pair, tiles, TILE, HEAD), jnp.bfloat16),
            pltpu.VMEM((8, members * rows), jnp.float32),
        ],
        in_specs=[hbm] * len(sources),
        out_specs=[whole, whole],
        scratch_shapes=[
            pltpu.SMEM(noise_levels.shape, jnp.int32),
            pltpu.SMEM(group_ids.shape, jnp.int32),
            pltpu.VMEM((gate_table.shape[0], pair * HEAD), jnp.float32),
            pltpu.SemaphoreType.DMA((3 + 3 * tiles,)),
        ],
    )(*(pltpu.with_memory_space_constraint(source, pltpu.HBM) for source in sources))
    own = exchanged(packed.reshape(members, 3 * pair * rows, HEAD))
    other = lax.ppermute(own, "group", [(0, 1), (1, 0)])
    done = pl.pallas_call(
        attend_kernel,
        out_shape=pltpu.VMEM((members, pair, rows, HEAD), jnp.bfloat16),
        in_specs=[whole] * 3,
        out_specs=whole,
    )(in_vmem(side), in_vmem(own), in_vmem(other))
    returned = exchanged(done.reshape(members, pair * rows, HEAD))
    handed = pl.pallas_call(
        unpack_kernel,
        out_shape=pltpu.HBM((tiles, members, pair, TILE, HEAD), jnp.bfloat16),
        in_specs=[whole],
        out_specs=hbm,
        scratch_shapes=[pltpu.SemaphoreType.DMA((tiles,))],
    )(in_vmem(returned.reshape(members, pair, tiles, TILE, HEAD)))
    return handed.transpose(0, 3, 1, 2, 4).reshape(rows, HEADS * HEAD)


def shifted(block, axis, distance):
    devices = range(lax.axis_size(axis))
    route = [((i - distance) % len(devices), i) for i in devices]
    return lax.ppermute(block, axis, route)


def doubled(states):
    row_count = states.shape[0]
    shaped = states.reshape(row_count, HEADS, 1, HEAD)
    return jnp.broadcast_to(shaped, (row_count, HEADS, 2, HEAD)).reshape(row_count, 2 * HEADS, HEAD)


def attend(running, chosen, key_block, value_block, key_group, group_ids, own_id):
    peak, total, summed = running
    marked = key_group[:, None] == jnp.arange(group_ids.shape[0], dtype=jnp.int32)[None, :]
    key_ids = jnp.sum(jnp.where(marked, group_ids[None, :], 0), axis=1)
    allowed = (key_ids <= own_id)[None, None, :]
    scores = jnp.einsum("pqd,rpd->pqr", chosen, key_block, preferred_element_type=jnp.float32)
    scores = jnp.where(allowed, scores * (1.0 / HEAD**0.5), -1e30)
    new_peak = jnp.maximum(peak, jnp.max(scores, axis=-1))
    weights = jnp.where(allowed, jnp.exp(scores - new_peak[..., None]), 0.0)
    total = jnp.sum(weights, axis=-1)
    summed = jnp.einsum(
        "pqr,rpd->pqd",
        weights.astype(jnp.bfloat16),
        value_block,
        preferred_element_type=jnp.float32,
    )
    return (new_peak, total, summed)


def local_wide(queries, key_states, value_states, gate_table, noise_levels, group_ids):
    tok_count = queries.shape[0]
    ctx_count = lax.axis_size("ctx")
    group_count = lax.axis_size("group")
    slot_count = 2 * HEADS // ctx_count
    group_rows = tok_count * ctx_count
    half_rows = group_rows // 2
    section_marks = jnp.arange(group_count, dtype=jnp.int32) == lax.axis_index("group")
    own_id = jnp.sum(jnp.where(section_marks, group_ids, 0))
    own_level = jnp.sum(jnp.where(section_marks, noise_levels, 0))
    slot_index = lax.axis_index("ctx") * slot_count + jnp.arange(slot_count, dtype=jnp.int32)
    offsets = slot_index % 2 * half_rows

    def select(offset, block):
        return lax.dynamic_slice_in_dim(block, offset, half_rows, 0)

    initial = (
        jnp.full((slot_count, half_rows), -1e30, jnp.float32),
        jnp.zeros((slot_count, half_rows), jnp.float32),
        jnp.zeros((slot_count, half_rows, HEAD), jnp.float32),
    )
    query_heads, key_heads, value_heads = (
        lax.all_to_all(doubled(queries), "ctx", split_axis=1, concat_axis=0, tiled=True),
        lax.all_to_all(doubled(key_states), "ctx", split_axis=1, concat_axis=0, tiled=True),
        lax.all_to_all(doubled(value_states), "ctx", split_axis=1, concat_axis=0, tiled=True),
    )
    chosen = jax.vmap(select, in_axes=(0, 1))(offsets, query_heads)
    key_piece = lax.all_gather(key_heads, "group", axis=0, tiled=True)
    value_piece = lax.all_gather(value_heads, "group", axis=0, tiled=True)
    key_group = jnp.arange(key_piece.shape[0], dtype=jnp.int32) // group_rows
    running = attend(initial, chosen, key_piece, value_piece, key_group, group_ids, own_id)
    peak, total, summed = running
    attended = (summed / total[..., None]).astype(jnp.bfloat16)

    def place(offset, block):
        return lax.dynamic_update_slice_in_dim(
            jnp.zeros((group_rows, HEAD), jnp.bfloat16), block, offset, 0
        )

    spread = jax.vmap(place, out_axes=1)(offsets, attended)
    returned = lax.all_to_all(spread, "ctx", split_axis=0, concat_axis=1, tiled=True)
    paired = returned.reshape(tok_count, HEADS, 2, HEAD)
    merged = (paired[:, :, 0] + paired[:, :, 1]).reshape(tok_count, HEADS * HEAD)
    level_marks = jnp.arange(gate_table.shape[0], dtype=jnp.int32)[:, None] == own_level
    gate_row = jnp.sum(jnp.where(level_marks, gate_table, 0.0), axis=0)
    done = (merged.astype(jnp.float32) * gate_row[None, :]).astype(jnp.bfloat16)
    return shifted(done, "group", 1)


def solution(mesh):
    in_pairs = mesh.shape["group"] == 2 and 2 * mesh.shape["ctx"] == HEADS
    tokens = P(("group", "ctx"), None)
    return jax.shard_map(
        local if in_pairs else local_wide,
        mesh=mesh,
        in_specs=(tokens, tokens, tokens, P(), P(), P()),
        out_specs=tokens,
        check_vma=False,
    )
```

```python
import functools

import jax
import jax.numpy as jnp
from jax import lax
from jax.experimental import pallas as pl
from jax.experimental.pallas import tpu as pltpu
from jax.sharding import PartitionSpec as P

HEADS = 32
HEAD = 128
LOG2_E = 1.4426950408889634
TILE = 8
FIRST = 11
SWAPPED = (0,)


def teams(members):
    order = [place ^ FIRST for place in range(members)]
    return [[(team ^ (member in SWAPPED)) * members + member for member in order] for team in range(2)]


def own_team():
    team = lax.axis_index("group")
    for member in SWAPPED:
        team = jnp.where(lax.axis_index("ctx") == member, 1 - team, team)
    return team


def pack_kernel(
    levels_ref, ids_ref, gate_ref, query_ref, key_ref, value_ref,
    packed_ref, side_ref, levels, ids, gate_block, sems,
):
    width = gate_block.shape[1]
    place = lax.axis_index("ctx") ^ FIRST
    columns = pl.ds(pl.multiple_of(place * width, width), width)
    pairs = []
    for part, ref in enumerate((query_ref, key_ref, value_ref)):
        for tile in range(ref.shape[0]):
            pairs.append((ref.at[tile], packed_ref.at[:, part, :, tile]))
    count = len(pairs)
    pairs += [(levels_ref, levels), (ids_ref, ids), (gate_ref.at[:, columns], gate_block)]
    fetches = [pltpu.make_async_copy(*pair, sems.at[i]) for i, pair in enumerate(pairs)]
    for fetch in fetches:
        fetch.start()
    for fetch in fetches[count:]:
        fetch.wait()
    own = own_team()
    other = 1 - own
    level_rows = lax.broadcasted_iota(jnp.int32, gate_block.shape, 0)

    def gate(group):
        return jnp.sum(jnp.where(level_rows == levels[group], gate_block[...], 0.0), axis=0, keepdims=True)

    keys = side_ref.shape[1]
    key_place = lax.broadcasted_iota(jnp.int32, (1, keys), 1) // (keys // packed_ref.shape[0])
    key_swapped = functools.reduce(jnp.logical_or, [key_place == member ^ FIRST for member in SWAPPED])
    straight = jnp.where(ids[own] <= ids[other], 0.0, -1e30)
    crossed = jnp.where(ids[other] <= ids[own], 0.0, -1e30)
    masks = [
        jnp.where(key_swapped, 0.0, straight),
        jnp.where(key_swapped, straight, 0.0),
        jnp.where(key_swapped, crossed, 0.0),
        jnp.where(key_swapped, 0.0, crossed),
    ]
    side_ref[pl.ds(0, 6), :] = jnp.concatenate([gate(other), gate(own), *masks], axis=0)
    for fetch in fetches[:count]:
        fetch.wait()


def attend_kernel(side_ref, own_ref, other_ref, out_ref):
    members, pair, rows, _ = out_ref.shape
    group_rows = members * rows
    factor = LOG2_E / HEAD**0.5
    swapped = [place ^ FIRST in SWAPPED for place in range(members)]
    cuts = [0, *(place for place in range(1, members) if swapped[place] != swapped[place - 1]), members]
    runs = [(slice(start * rows, stop * rows), swapped[start]) for start, stop in zip(cuts, cuts[1:])]

    def tokens(ref, part, head):
        return ref[:, pl.ds((part * pair + head) * rows, rows), :].reshape(group_rows, HEAD)

    def dot(a, b, contract):
        return lax.dot_general(a, b, ((contract[:1], contract[1:]), ((), ())), preferred_element_type=jnp.float32)

    def masked(score, side):
        masks = [side_ref[2 + 2 * kind + side : 3 + 2 * kind + side, :] for kind in range(2)]
        return jnp.concatenate([score[run] + masks[kind] for run, kind in runs], axis=0)

    ones = jnp.ones((group_rows, HEAD), jnp.bfloat16)
    for head in range(pair):
        queries = tokens(other_ref, 0, head)
        refs = (own_ref, other_ref)
        scores = [masked(dot(queries, tokens(ref, 1, head), (1, 1)), side) for side, ref in enumerate(refs)]
        peak = jnp.max(jnp.maximum(*scores), axis=1, keepdims=True)
        weights = [jnp.exp2((score - peak) * factor).astype(jnp.bfloat16) for score in scores]
        values = [jnp.concatenate([tokens(ref, 2, head), ones], axis=1) for ref in refs]
        summed = sum(dot(weight, value, (1, 0)) for weight, value in zip(weights, values))
        attended = (summed[:, :HEAD] / summed[:, HEAD:]).astype(jnp.bfloat16).astype(jnp.float32)
        gates = [side_ref[kind : kind + 1, head * HEAD : (head + 1) * HEAD] for kind in range(2)]
        done = jnp.concatenate([attended[run] * gates[kind] for run, kind in runs], axis=0).astype(jnp.bfloat16)
        out_ref[:, head] = done.reshape(members, rows, HEAD)


def unpack_kernel(heads_ref, out_ref, sems):
    copies = [
        pltpu.make_async_copy(heads_ref.at[:, :, tile], out_ref.at[tile], sems.at[tile])
        for tile in range(out_ref.shape[0])
    ]
    for copy in copies:
        copy.start()
    for copy in copies:
        copy.wait()


def in_vmem(array):
    return pltpu.with_memory_space_constraint(array, pltpu.VMEM)


def tiled(states, members):
    rows, columns = states.shape
    pair = columns // HEAD // members
    return states.reshape(rows // TILE, TILE, members, pair, HEAD).transpose(0, 2, 3, 1, 4)


def exchanged(chunks):
    groups = teams(chunks.shape[0])
    return lax.all_to_all(chunks, ("group", "ctx"), split_axis=0, concat_axis=0, tiled=True, axis_index_groups=groups)


def local(queries, key_states, value_states, gate_table, noise_levels, group_ids):
    rows = queries.shape[0]
    tiles = rows // TILE
    members = lax.axis_size("ctx")
    pair = HEADS // members
    whole = pl.BlockSpec(memory_space=pltpu.VMEM)
    hbm = pl.BlockSpec(memory_space=pltpu.HBM)
    states = (tiled(array, members) for array in (queries, key_states, value_states))
    sources = (noise_levels, group_ids, gate_table, *states)
    packed, side = pl.pallas_call(
        pack_kernel,
        out_shape=[
            pltpu.VMEM((members, 3, pair, tiles, TILE, HEAD), jnp.bfloat16),
            pltpu.VMEM((8, members * rows), jnp.float32),
        ],
        in_specs=[hbm] * len(sources),
        out_specs=[whole, whole],
        scratch_shapes=[
            pltpu.SMEM(noise_levels.shape, jnp.int32),
            pltpu.SMEM(group_ids.shape, jnp.int32),
            pltpu.VMEM((gate_table.shape[0], pair * HEAD), jnp.float32),
            pltpu.SemaphoreType.DMA((3 + 3 * tiles,)),
        ],
    )(*(pltpu.with_memory_space_constraint(source, pltpu.HBM) for source in sources))
    own = exchanged(packed.reshape(members, 3 * pair * rows, HEAD))
    other = lax.ppermute(own, "group", [(0, 1), (1, 0)])
    done = pl.pallas_call(
        attend_kernel,
        out_shape=pltpu.VMEM((members, pair, rows, HEAD), jnp.bfloat16),
        in_specs=[whole] * 3,
        out_specs=whole,
    )(in_vmem(side), in_vmem(own), in_vmem(other))
    returned = exchanged(done.reshape(members, pair * rows, HEAD))
    handed = pl.pallas_call(
        unpack_kernel,
        out_shape=pltpu.HBM((tiles, members, pair, TILE, HEAD), jnp.bfloat16),
        in_specs=[whole],
        out_specs=hbm,
        scratch_shapes=[pltpu.SemaphoreType.DMA((tiles,))],
    )(in_vmem(returned.reshape(members, pair, tiles, TILE, HEAD)))
    return handed.transpose(0, 3, 1, 2, 4).reshape(rows, HEADS * HEAD)


def shifted(block, axis, distance):
    devices = range(lax.axis_size(axis))
    route = [((i - distance) % len(devices), i) for i in devices]
    return lax.ppermute(block, axis, route)


def doubled(states):
    row_count = states.shape[0]
    shaped = states.reshape(row_count, HEADS, 1, HEAD)
    return jnp.broadcast_to(shaped, (row_count, HEADS, 2, HEAD)).reshape(row_count, 2 * HEADS, HEAD)


def attend(running, chosen, key_block, value_block, key_group, group_ids, own_id):
    peak, total, summed = running
    marked = key_group[:, None] == jnp.arange(group_ids.shape[0], dtype=jnp.int32)[None, :]
    key_ids = jnp.sum(jnp.where(marked, group_ids[None, :], 0), axis=1)
    allowed = (key_ids <= own_id)[None, None, :]
    scores = jnp.einsum("pqd,rpd->pqr", chosen, key_block, preferred_element_type=jnp.float32)
    scores = jnp.where(allowed, scores * (1.0 / HEAD**0.5), -1e30)
    new_peak = jnp.maximum(peak, jnp.max(scores, axis=-1))
    weights = jnp.where(allowed, jnp.exp(scores - new_peak[..., None]), 0.0)
    total = jnp.sum(weights, axis=-1)
    summed = jnp.einsum(
        "pqr,rpd->pqd",
        weights.astype(jnp.bfloat16),
        value_block,
        preferred_element_type=jnp.float32,
    )
    return (new_peak, total, summed)


def local_wide(queries, key_states, value_states, gate_table, noise_levels, group_ids):
    tok_count = queries.shape[0]
    ctx_count = lax.axis_size("ctx")
    group_count = lax.axis_size("group")
    slot_count = 2 * HEADS // ctx_count
    group_rows = tok_count * ctx_count
    half_rows = group_rows // 2
    section_marks = jnp.arange(group_count, dtype=jnp.int32) == lax.axis_index("group")
    own_id = jnp.sum(jnp.where(section_marks, group_ids, 0))
    own_level = jnp.sum(jnp.where(section_marks, noise_levels, 0))
    slot_index = lax.axis_index("ctx") * slot_count + jnp.arange(slot_count, dtype=jnp.int32)
    offsets = slot_index % 2 * half_rows

    def select(offset, block):
        return lax.dynamic_slice_in_dim(block, offset, half_rows, 0)

    initial = (
        jnp.full((slot_count, half_rows), -1e30, jnp.float32),
        jnp.zeros((slot_count, half_rows), jnp.float32),
        jnp.zeros((slot_count, half_rows, HEAD), jnp.float32),
    )
    query_heads, key_heads, value_heads = (
        lax.all_to_all(doubled(queries), "ctx", split_axis=1, concat_axis=0, tiled=True),
        lax.all_to_all(doubled(key_states), "ctx", split_axis=1, concat_axis=0, tiled=True),
        lax.all_to_all(doubled(value_states), "ctx", split_axis=1, concat_axis=0, tiled=True),
    )
    chosen = jax.vmap(select, in_axes=(0, 1))(offsets, query_heads)
    key_piece = lax.all_gather(key_heads, "group", axis=0, tiled=True)
    value_piece = lax.all_gather(value_heads, "group", axis=0, tiled=True)
    key_group = jnp.arange(key_piece.shape[0], dtype=jnp.int32) // group_rows
    running = attend(initial, chosen, key_piece, value_piece, key_group, group_ids, own_id)
    peak, total, summed = running
    attended = (summed / total[..., None]).astype(jnp.bfloat16)

    def place(offset, block):
        return lax.dynamic_update_slice_in_dim(
            jnp.zeros((group_rows, HEAD), jnp.bfloat16), block, offset, 0
        )

    spread = jax.vmap(place, out_axes=1)(offsets, attended)
    returned = lax.all_to_all(spread, "ctx", split_axis=0, concat_axis=1, tiled=True)
    paired = returned.reshape(tok_count, HEADS, 2, HEAD)
    merged = (paired[:, :, 0] + paired[:, :, 1]).reshape(tok_count, HEADS * HEAD)
    level_marks = jnp.arange(gate_table.shape[0], dtype=jnp.int32)[:, None] == own_level
    gate_row = jnp.sum(jnp.where(level_marks, gate_table, 0.0), axis=0)
    done = (merged.astype(jnp.float32) * gate_row[None, :]).astype(jnp.bfloat16)
    return shifted(done, "group", 1)


def solution(mesh):
    in_pairs = mesh.shape["group"] == 2 and 2 * mesh.shape["ctx"] == HEADS
    tokens = P(("group", "ctx"), None)
    return jax.shard_map(
        local if in_pairs else local_wide,
        mesh=mesh,
        in_specs=(tokens, tokens, tokens, P(), P(), P()),
        out_specs=tokens,
        check_vma=False,
    )
```

```python
import functools

import jax
import jax.numpy as jnp
from jax import lax
from jax.experimental import pallas as pl
from jax.experimental.pallas import tpu as pltpu
from jax.sharding import PartitionSpec as P

HEADS = 32
HEAD = 128
LOG2_E = 1.4426950408889634
TILE = 8
FIRST = 11
SWAPPED = (0,)


def teams(members):
    order = [place ^ FIRST for place in range(members)]
    return [[(team ^ (member in SWAPPED)) * members + member for member in order] for team in range(2)]


def own_team():
    team = lax.axis_index("group")
    for member in SWAPPED:
        team = jnp.where(lax.axis_index("ctx") == member, 1 - team, team)
    return team


def pack_kernel(
    levels_ref, ids_ref, gate_ref, query_ref, key_ref, value_ref,
    packed_ref, side_ref, levels, ids, gate_block, sems,
):
    width = gate_block.shape[1]
    place = lax.axis_index("ctx") ^ FIRST
    columns = pl.ds(pl.multiple_of(place * width, width), width)
    pairs = [(levels_ref, levels), (ids_ref, ids), (gate_ref.at[:, columns], gate_block)]
    for part, ref in enumerate((query_ref, key_ref, value_ref)):
        for tile in range(ref.shape[0]):
            pairs.append((ref.at[tile], packed_ref.at[:, part, :, tile]))
    fetches = [pltpu.make_async_copy(*pair, sems.at[i]) for i, pair in enumerate(pairs)]
    for fetch in fetches:
        fetch.start()
    for fetch in fetches[:3]:
        fetch.wait()
    own = own_team()
    other = 1 - own
    level_rows = lax.broadcasted_iota(jnp.int32, gate_block.shape, 0)

    def gate(group):
        return jnp.sum(jnp.where(level_rows == levels[group], gate_block[...], 0.0), axis=0, keepdims=True)

    keys = side_ref.shape[1]
    key_place = lax.broadcasted_iota(jnp.int32, (1, keys), 1) // (keys // packed_ref.shape[0])
    key_swapped = functools.reduce(jnp.logical_or, [key_place == member ^ FIRST for member in SWAPPED])
    straight = jnp.where(ids[own] <= ids[other], 0.0, -1e30)
    crossed = jnp.where(ids[other] <= ids[own], 0.0, -1e30)
    masks = [
        jnp.where(key_swapped, 0.0, straight),
        jnp.where(key_swapped, straight, 0.0),
        jnp.where(key_swapped, crossed, 0.0),
        jnp.where(key_swapped, 0.0, crossed),
    ]
    side_ref[pl.ds(0, 6), :] = jnp.concatenate([gate(other), gate(own), *masks], axis=0)
    for fetch in fetches[3:]:
        fetch.wait()


def attend_kernel(side_ref, own_ref, other_ref, out_ref):
    members, pair, rows, _ = out_ref.shape
    group_rows = members * rows
    factor = LOG2_E / HEAD**0.5
    swapped = [place ^ FIRST in SWAPPED for place in range(members)]
    cuts = [0, *(place for place in range(1, members) if swapped[place] != swapped[place - 1]), members]
    runs = [(slice(start * rows, stop * rows), swapped[start]) for start, stop in zip(cuts, cuts[1:])]

    def tokens(ref, part, head):
        return ref[:, pl.ds((part * pair + head) * rows, rows), :].reshape(group_rows, HEAD)

    def dot(a, b, contract):
        return lax.dot_general(a, b, ((contract[:1], contract[1:]), ((), ())), preferred_element_type=jnp.float32)

    def masked(score, side):
        masks = [side_ref[2 + 2 * kind + side : 3 + 2 * kind + side, :] for kind in range(2)]
        return jnp.concatenate([score[run] + masks[kind] for run, kind in runs], axis=0)

    ones = jnp.ones((group_rows, HEAD), jnp.bfloat16)
    refs = (own_ref, other_ref)
    scores = [
        [dot(tokens(other_ref, 0, head), tokens(ref, 1, head), (1, 1)) for ref in refs] for head in range(pair)
    ]
    summed = []
    for head in range(pair):
        blocks = [masked(score, side) for side, score in enumerate(scores[head])]
        peak = jnp.max(jnp.maximum(*blocks), axis=1, keepdims=True)
        weights = [jnp.exp2((block - peak) * factor).astype(jnp.bfloat16) for block in blocks]
        values = [jnp.concatenate([tokens(ref, 2, head), ones], axis=1) for ref in refs]
        summed.append(sum(dot(weight, value, (1, 0)) for weight, value in zip(weights, values)))
    for head in range(pair):
        attended = (summed[head][:, :HEAD] / summed[head][:, HEAD:]).astype(jnp.bfloat16).astype(jnp.float32)
        gates = [side_ref[kind : kind + 1, head * HEAD : (head + 1) * HEAD] for kind in range(2)]
        done = jnp.concatenate([attended[run] * gates[kind] for run, kind in runs], axis=0).astype(jnp.bfloat16)
        out_ref[:, head] = done.reshape(members, rows, HEAD)


def unpack_kernel(heads_ref, out_ref, sems):
    copies = [
        pltpu.make_async_copy(heads_ref.at[:, :, tile], out_ref.at[tile], sems.at[tile])
        for tile in range(out_ref.shape[0])
    ]
    for copy in copies:
        copy.start()
    for copy in copies:
        copy.wait()


def in_vmem(array):
    return pltpu.with_memory_space_constraint(array, pltpu.VMEM)


def tiled(states, members):
    rows, columns = states.shape
    pair = columns // HEAD // members
    return states.reshape(rows // TILE, TILE, members, pair, HEAD).transpose(0, 2, 3, 1, 4)


def exchanged(chunks):
    groups = teams(chunks.shape[0])
    return lax.all_to_all(chunks, ("group", "ctx"), split_axis=0, concat_axis=0, tiled=True, axis_index_groups=groups)


def local(queries, key_states, value_states, gate_table, noise_levels, group_ids):
    rows = queries.shape[0]
    tiles = rows // TILE
    members = lax.axis_size("ctx")
    pair = HEADS // members
    whole = pl.BlockSpec(memory_space=pltpu.VMEM)
    hbm = pl.BlockSpec(memory_space=pltpu.HBM)
    states = (tiled(array, members) for array in (queries, key_states, value_states))
    sources = (noise_levels, group_ids, gate_table, *states)
    packed, side = pl.pallas_call(
        pack_kernel,
        out_shape=[
            pltpu.VMEM((members, 3, pair, tiles, TILE, HEAD), jnp.bfloat16),
            pltpu.VMEM((8, members * rows), jnp.float32),
        ],
        in_specs=[hbm] * len(sources),
        out_specs=[whole, whole],
        scratch_shapes=[
            pltpu.SMEM(noise_levels.shape, jnp.int32),
            pltpu.SMEM(group_ids.shape, jnp.int32),
            pltpu.VMEM((gate_table.shape[0], pair * HEAD), jnp.float32),
            pltpu.SemaphoreType.DMA((3 + 3 * tiles,)),
        ],
    )(*(pltpu.with_memory_space_constraint(source, pltpu.HBM) for source in sources))
    own = exchanged(packed.reshape(members, 3 * pair * rows, HEAD))
    other = lax.ppermute(own, "group", [(0, 1), (1, 0)])
    done = pl.pallas_call(
        attend_kernel,
        out_shape=pltpu.VMEM((members, pair, rows, HEAD), jnp.bfloat16),
        in_specs=[whole] * 3,
        out_specs=whole,
    )(in_vmem(side), in_vmem(own), in_vmem(other))
    returned = exchanged(done.reshape(members, pair * rows, HEAD))
    handed = pl.pallas_call(
        unpack_kernel,
        out_shape=pltpu.HBM((tiles, members, pair, TILE, HEAD), jnp.bfloat16),
        in_specs=[whole],
        out_specs=hbm,
        scratch_shapes=[pltpu.SemaphoreType.DMA((tiles,))],
    )(in_vmem(returned.reshape(members, pair, tiles, TILE, HEAD)))
    return handed.transpose(0, 3, 1, 2, 4).reshape(rows, HEADS * HEAD)


def shifted(block, axis, distance):
    devices = range(lax.axis_size(axis))
    route = [((i - distance) % len(devices), i) for i in devices]
    return lax.ppermute(block, axis, route)


def doubled(states):
    row_count = states.shape[0]
    shaped = states.reshape(row_count, HEADS, 1, HEAD)
    return jnp.broadcast_to(shaped, (row_count, HEADS, 2, HEAD)).reshape(row_count, 2 * HEADS, HEAD)


def attend(running, chosen, key_block, value_block, key_group, group_ids, own_id):
    peak, total, summed = running
    marked = key_group[:, None] == jnp.arange(group_ids.shape[0], dtype=jnp.int32)[None, :]
    key_ids = jnp.sum(jnp.where(marked, group_ids[None, :], 0), axis=1)
    allowed = (key_ids <= own_id)[None, None, :]
    scores = jnp.einsum("pqd,rpd->pqr", chosen, key_block, preferred_element_type=jnp.float32)
    scores = jnp.where(allowed, scores * (1.0 / HEAD**0.5), -1e30)
    new_peak = jnp.maximum(peak, jnp.max(scores, axis=-1))
    weights = jnp.where(allowed, jnp.exp(scores - new_peak[..., None]), 0.0)
    total = jnp.sum(weights, axis=-1)
    summed = jnp.einsum(
        "pqr,rpd->pqd",
        weights.astype(jnp.bfloat16),
        value_block,
        preferred_element_type=jnp.float32,
    )
    return (new_peak, total, summed)


def local_wide(queries, key_states, value_states, gate_table, noise_levels, group_ids):
    tok_count = queries.shape[0]
    ctx_count = lax.axis_size("ctx")
    group_count = lax.axis_size("group")
    slot_count = 2 * HEADS // ctx_count
    group_rows = tok_count * ctx_count
    half_rows = group_rows // 2
    section_marks = jnp.arange(group_count, dtype=jnp.int32) == lax.axis_index("group")
    own_id = jnp.sum(jnp.where(section_marks, group_ids, 0))
    own_level = jnp.sum(jnp.where(section_marks, noise_levels, 0))
    slot_index = lax.axis_index("ctx") * slot_count + jnp.arange(slot_count, dtype=jnp.int32)
    offsets = slot_index % 2 * half_rows

    def select(offset, block):
        return lax.dynamic_slice_in_dim(block, offset, half_rows, 0)

    initial = (
        jnp.full((slot_count, half_rows), -1e30, jnp.float32),
        jnp.zeros((slot_count, half_rows), jnp.float32),
        jnp.zeros((slot_count, half_rows, HEAD), jnp.float32),
    )
    query_heads, key_heads, value_heads = (
        lax.all_to_all(doubled(queries), "ctx", split_axis=1, concat_axis=0, tiled=True),
        lax.all_to_all(doubled(key_states), "ctx", split_axis=1, concat_axis=0, tiled=True),
        lax.all_to_all(doubled(value_states), "ctx", split_axis=1, concat_axis=0, tiled=True),
    )
    chosen = jax.vmap(select, in_axes=(0, 1))(offsets, query_heads)
    key_piece = lax.all_gather(key_heads, "group", axis=0, tiled=True)
    value_piece = lax.all_gather(value_heads, "group", axis=0, tiled=True)
    key_group = jnp.arange(key_piece.shape[0], dtype=jnp.int32) // group_rows
    running = attend(initial, chosen, key_piece, value_piece, key_group, group_ids, own_id)
    peak, total, summed = running
    attended = (summed / total[..., None]).astype(jnp.bfloat16)

    def place(offset, block):
        return lax.dynamic_update_slice_in_dim(
            jnp.zeros((group_rows, HEAD), jnp.bfloat16), block, offset, 0
        )

    spread = jax.vmap(place, out_axes=1)(offsets, attended)
    returned = lax.all_to_all(spread, "ctx", split_axis=0, concat_axis=1, tiled=True)
    paired = returned.reshape(tok_count, HEADS, 2, HEAD)
    merged = (paired[:, :, 0] + paired[:, :, 1]).reshape(tok_count, HEADS * HEAD)
    level_marks = jnp.arange(gate_table.shape[0], dtype=jnp.int32)[:, None] == own_level
    gate_row = jnp.sum(jnp.where(level_marks, gate_table, 0.0), axis=0)
    done = (merged.astype(jnp.float32) * gate_row[None, :]).astype(jnp.bfloat16)
    return shifted(done, "group", 1)


def solution(mesh):
    in_pairs = mesh.shape["group"] == 2 and 2 * mesh.shape["ctx"] == HEADS
    tokens = P(("group", "ctx"), None)
    return jax.shard_map(
        local if in_pairs else local_wide,
        mesh=mesh,
        in_specs=(tokens, tokens, tokens, P(), P(), P()),
        out_specs=tokens,
        check_vma=False,
    )
```

```python
import functools

import jax
import jax.numpy as jnp
from jax import lax
from jax.experimental import pallas as pl
from jax.experimental.pallas import tpu as pltpu
from jax.sharding import PartitionSpec as P

HEADS = 32
HEAD = 128
LOG2_E = 1.4426950408889634
TILE = 8
FIRST = 11
SWAPPED = (0,)


def teams(members):
    order = [place ^ FIRST for place in range(members)]
    return [[(team ^ (member in SWAPPED)) * members + member for member in order] for team in range(2)]


def own_team():
    team = lax.axis_index("group")
    for member in SWAPPED:
        team = jnp.where(lax.axis_index("ctx") == member, 1 - team, team)
    return team


def pack_kernel(
    levels_ref, ids_ref, gate_ref, query_ref, key_ref, value_ref,
    packed_ref, side_ref, levels, ids, gate_block, sems,
):
    width = gate_block.shape[1]
    place = lax.axis_index("ctx") ^ FIRST
    columns = pl.ds(pl.multiple_of(place * width, width), width)
    pairs = []
    for part, ref in enumerate((query_ref, key_ref, value_ref)):
        for tile in range(ref.shape[0]):
            pairs.append((ref.at[tile], packed_ref.at[:, part, :, tile]))
    count = len(pairs)
    pairs += [(levels_ref, levels), (ids_ref, ids), (gate_ref.at[:, columns], gate_block)]
    fetches = [pltpu.make_async_copy(*pair, sems.at[i]) for i, pair in enumerate(pairs)]
    for fetch in fetches:
        fetch.start()
    for fetch in fetches[count:]:
        fetch.wait()
    own = own_team()
    other = 1 - own
    level_rows = lax.broadcasted_iota(jnp.int32, gate_block.shape, 0)

    def gate(group):
        return jnp.sum(jnp.where(level_rows == levels[group], gate_block[...], 0.0), axis=0, keepdims=True)

    keys = side_ref.shape[1]
    key_place = lax.broadcasted_iota(jnp.int32, (1, keys), 1) // (keys // packed_ref.shape[0])
    key_swapped = functools.reduce(jnp.logical_or, [key_place == member ^ FIRST for member in SWAPPED])
    straight = jnp.where(ids[own] <= ids[other], 0.0, -1e30)
    crossed = jnp.where(ids[other] <= ids[own], 0.0, -1e30)
    masks = [
        jnp.where(key_swapped, 0.0, straight),
        jnp.where(key_swapped, straight, 0.0),
        jnp.where(key_swapped, crossed, 0.0),
        jnp.where(key_swapped, 0.0, crossed),
    ]
    side_ref[pl.ds(0, 6), :] = jnp.concatenate([gate(other), gate(own), *masks], axis=0)
    for fetch in fetches[:count]:
        fetch.wait()


def attend_kernel(side_ref, own_ref, other_ref, out_ref):
    members, pair, rows, _ = out_ref.shape
    group_rows = members * rows
    factor = LOG2_E / HEAD**0.5
    swapped = [place ^ FIRST in SWAPPED for place in range(members)]
    cuts = [0, *(place for place in range(1, members) if swapped[place] != swapped[place - 1]), members]
    runs = [(slice(start * rows, stop * rows), swapped[start]) for start, stop in zip(cuts, cuts[1:])]

    def tokens(ref, part, head):
        return ref[:, pl.ds((part * pair + head) * rows, rows), :].reshape(group_rows, HEAD)

    def dot(a, b, contract):
        return lax.dot_general(a, b, ((contract[:1], contract[1:]), ((), ())), preferred_element_type=jnp.float32)

    def masked(score, side):
        masks = [side_ref[2 + 2 * kind + side : 3 + 2 * kind + side, :] for kind in range(2)]
        return jnp.concatenate([score[run] + masks[kind] for run, kind in runs], axis=0)

    ones = jnp.ones((group_rows, HEAD), jnp.bfloat16)
    refs = (own_ref, other_ref)
    scores = [
        [dot(tokens(other_ref, 0, head), tokens(ref, 1, head), (1, 1)) for ref in refs] for head in range(pair)
    ]
    weights = []
    for head in range(pair):
        blocks = [masked(score, side) for side, score in enumerate(scores[head])]
        peak = jnp.max(jnp.maximum(*blocks), axis=1, keepdims=True)
        weights.append([jnp.exp2((block - peak) * factor).astype(jnp.bfloat16) for block in blocks])
    summed = []
    for head in range(pair):
        values = [jnp.concatenate([tokens(ref, 2, head), ones], axis=1) for ref in refs]
        summed.append(sum(dot(weight, value, (1, 0)) for weight, value in zip(weights[head], values)))
    for head in range(pair):
        attended = (summed[head][:, :HEAD] / summed[head][:, HEAD:]).astype(jnp.bfloat16).astype(jnp.float32)
        gates = [side_ref[kind : kind + 1, head * HEAD : (head + 1) * HEAD] for kind in range(2)]
        done = jnp.concatenate([attended[run] * gates[kind] for run, kind in runs], axis=0).astype(jnp.bfloat16)
        out_ref[:, head] = done.reshape(members, rows, HEAD)


def unpack_kernel(heads_ref, out_ref, sems):
    copies = [
        pltpu.make_async_copy(heads_ref.at[:, :, tile], out_ref.at[tile], sems.at[tile])
        for tile in range(out_ref.shape[0])
    ]
    for copy in copies:
        copy.start()
    for copy in copies:
        copy.wait()


def in_vmem(array):
    return pltpu.with_memory_space_constraint(array, pltpu.VMEM)


def tiled(states, members):
    rows, columns = states.shape
    pair = columns // HEAD // members
    return states.reshape(rows // TILE, TILE, members, pair, HEAD).transpose(0, 2, 3, 1, 4)


def exchanged(chunks):
    groups = teams(chunks.shape[0])
    return lax.all_to_all(chunks, ("group", "ctx"), split_axis=0, concat_axis=0, tiled=True, axis_index_groups=groups)


def local(queries, key_states, value_states, gate_table, noise_levels, group_ids):
    rows = queries.shape[0]
    tiles = rows // TILE
    members = lax.axis_size("ctx")
    pair = HEADS // members
    whole = pl.BlockSpec(memory_space=pltpu.VMEM)
    hbm = pl.BlockSpec(memory_space=pltpu.HBM)
    states = (tiled(array, members) for array in (queries, key_states, value_states))
    sources = (noise_levels, group_ids, gate_table, *states)
    packed, side = pl.pallas_call(
        pack_kernel,
        out_shape=[
            pltpu.VMEM((members, 3, pair, tiles, TILE, HEAD), jnp.bfloat16),
            pltpu.VMEM((8, members * rows), jnp.float32),
        ],
        in_specs=[hbm] * len(sources),
        out_specs=[whole, whole],
        scratch_shapes=[
            pltpu.SMEM(noise_levels.shape, jnp.int32),
            pltpu.SMEM(group_ids.shape, jnp.int32),
            pltpu.VMEM((gate_table.shape[0], pair * HEAD), jnp.float32),
            pltpu.SemaphoreType.DMA((3 + 3 * tiles,)),
        ],
    )(*(pltpu.with_memory_space_constraint(source, pltpu.HBM) for source in sources))
    own = exchanged(packed.reshape(members, 3 * pair * rows, HEAD))
    other = lax.ppermute(own, "group", [(0, 1), (1, 0)])
    done = pl.pallas_call(
        attend_kernel,
        out_shape=pltpu.VMEM((members, pair, rows, HEAD), jnp.bfloat16),
        in_specs=[whole] * 3,
        out_specs=whole,
    )(in_vmem(side), in_vmem(own), in_vmem(other))
    returned = exchanged(done.reshape(members, pair * rows, HEAD))
    handed = pl.pallas_call(
        unpack_kernel,
        out_shape=pltpu.HBM((tiles, members, pair, TILE, HEAD), jnp.bfloat16),
        in_specs=[whole],
        out_specs=hbm,
        scratch_shapes=[pltpu.SemaphoreType.DMA((tiles,))],
    )(in_vmem(returned.reshape(members, pair, tiles, TILE, HEAD)))
    return handed.transpose(0, 3, 1, 2, 4).reshape(rows, HEADS * HEAD)


def shifted(block, axis, distance):
    devices = range(lax.axis_size(axis))
    route = [((i - distance) % len(devices), i) for i in devices]
    return lax.ppermute(block, axis, route)


def doubled(states):
    row_count = states.shape[0]
    shaped = states.reshape(row_count, HEADS, 1, HEAD)
    return jnp.broadcast_to(shaped, (row_count, HEADS, 2, HEAD)).reshape(row_count, 2 * HEADS, HEAD)


def attend(running, chosen, key_block, value_block, key_group, group_ids, own_id):
    peak, total, summed = running
    marked = key_group[:, None] == jnp.arange(group_ids.shape[0], dtype=jnp.int32)[None, :]
    key_ids = jnp.sum(jnp.where(marked, group_ids[None, :], 0), axis=1)
    allowed = (key_ids <= own_id)[None, None, :]
    scores = jnp.einsum("pqd,rpd->pqr", chosen, key_block, preferred_element_type=jnp.float32)
    scores = jnp.where(allowed, scores * (1.0 / HEAD**0.5), -1e30)
    new_peak = jnp.maximum(peak, jnp.max(scores, axis=-1))
    weights = jnp.where(allowed, jnp.exp(scores - new_peak[..., None]), 0.0)
    total = jnp.sum(weights, axis=-1)
    summed = jnp.einsum(
        "pqr,rpd->pqd",
        weights.astype(jnp.bfloat16),
        value_block,
        preferred_element_type=jnp.float32,
    )
    return (new_peak, total, summed)


def local_wide(queries, key_states, value_states, gate_table, noise_levels, group_ids):
    tok_count = queries.shape[0]
    ctx_count = lax.axis_size("ctx")
    group_count = lax.axis_size("group")
    slot_count = 2 * HEADS // ctx_count
    group_rows = tok_count * ctx_count
    half_rows = group_rows // 2
    section_marks = jnp.arange(group_count, dtype=jnp.int32) == lax.axis_index("group")
    own_id = jnp.sum(jnp.where(section_marks, group_ids, 0))
    own_level = jnp.sum(jnp.where(section_marks, noise_levels, 0))
    slot_index = lax.axis_index("ctx") * slot_count + jnp.arange(slot_count, dtype=jnp.int32)
    offsets = slot_index % 2 * half_rows

    def select(offset, block):
        return lax.dynamic_slice_in_dim(block, offset, half_rows, 0)

    initial = (
        jnp.full((slot_count, half_rows), -1e30, jnp.float32),
        jnp.zeros((slot_count, half_rows), jnp.float32),
        jnp.zeros((slot_count, half_rows, HEAD), jnp.float32),
    )
    query_heads, key_heads, value_heads = (
        lax.all_to_all(doubled(queries), "ctx", split_axis=1, concat_axis=0, tiled=True),
        lax.all_to_all(doubled(key_states), "ctx", split_axis=1, concat_axis=0, tiled=True),
        lax.all_to_all(doubled(value_states), "ctx", split_axis=1, concat_axis=0, tiled=True),
    )
    chosen = jax.vmap(select, in_axes=(0, 1))(offsets, query_heads)
    key_piece = lax.all_gather(key_heads, "group", axis=0, tiled=True)
    value_piece = lax.all_gather(value_heads, "group", axis=0, tiled=True)
    key_group = jnp.arange(key_piece.shape[0], dtype=jnp.int32) // group_rows
    running = attend(initial, chosen, key_piece, value_piece, key_group, group_ids, own_id)
    peak, total, summed = running
    attended = (summed / total[..., None]).astype(jnp.bfloat16)

    def place(offset, block):
        return lax.dynamic_update_slice_in_dim(
            jnp.zeros((group_rows, HEAD), jnp.bfloat16), block, offset, 0
        )

    spread = jax.vmap(place, out_axes=1)(offsets, attended)
    returned = lax.all_to_all(spread, "ctx", split_axis=0, concat_axis=1, tiled=True)
    paired = returned.reshape(tok_count, HEADS, 2, HEAD)
    merged = (paired[:, :, 0] + paired[:, :, 1]).reshape(tok_count, HEADS * HEAD)
    level_marks = jnp.arange(gate_table.shape[0], dtype=jnp.int32)[:, None] == own_level
    gate_row = jnp.sum(jnp.where(level_marks, gate_table, 0.0), axis=0)
    done = (merged.astype(jnp.float32) * gate_row[None, :]).astype(jnp.bfloat16)
    return shifted(done, "group", 1)


def solution(mesh):
    in_pairs = mesh.shape["group"] == 2 and 2 * mesh.shape["ctx"] == HEADS
    tokens = P(("group", "ctx"), None)
    return jax.shard_map(
        local if in_pairs else local_wide,
        mesh=mesh,
        in_specs=(tokens, tokens, tokens, P(), P(), P()),
        out_specs=tokens,
        check_vma=False,
    )
```

```python
import functools

import jax
import jax.numpy as jnp
from jax import lax
from jax.experimental import pallas as pl
from jax.experimental.pallas import tpu as pltpu
from jax.sharding import PartitionSpec as P

HEADS = 32
HEAD = 128
LOG2_E = 1.4426950408889634
TILE = 8
FIRST = 11
SWAPPED = (0,)


def teams(members):
    order = [place ^ FIRST for place in range(members)]
    return [[(team ^ (member in SWAPPED)) * members + member for member in order] for team in range(2)]


def own_team():
    team = lax.axis_index("group")
    for member in SWAPPED:
        team = jnp.where(lax.axis_index("ctx") == member, 1 - team, team)
    return team


def halves(places):
    return [pl.ds(start, places // 2) for start in (0, places // 2)]


def pack_kernel(
    levels_ref, ids_ref, gate_ref, query_ref, key_ref, value_ref,
    packed_ref, side_ref, levels, ids, gate_block, sems,
):
    width = gate_block.shape[1]
    place = lax.axis_index("ctx") ^ FIRST
    columns = pl.ds(pl.multiple_of(place * width, width), width)
    pairs = []
    for part, ref in enumerate((query_ref, key_ref, value_ref)):
        for tile in range(ref.shape[0]):
            for half in halves(packed_ref.shape[0]):
                pairs.append((ref.at[tile, half], packed_ref.at[half, part, :, tile]))
    count = len(pairs)
    pairs += [(levels_ref, levels), (ids_ref, ids), (gate_ref.at[:, columns], gate_block)]
    fetches = [pltpu.make_async_copy(*pair, sems.at[i]) for i, pair in enumerate(pairs)]
    for fetch in fetches:
        fetch.start()
    for fetch in fetches[count:]:
        fetch.wait()
    own = own_team()
    other = 1 - own
    level_rows = lax.broadcasted_iota(jnp.int32, gate_block.shape, 0)

    def gate(group):
        return jnp.sum(jnp.where(level_rows == levels[group], gate_block[...], 0.0), axis=0, keepdims=True)

    keys = side_ref.shape[1]
    key_place = lax.broadcasted_iota(jnp.int32, (1, keys), 1) // (keys // packed_ref.shape[0])
    key_swapped = functools.reduce(jnp.logical_or, [key_place == member ^ FIRST for member in SWAPPED])
    straight = jnp.where(ids[own] <= ids[other], 0.0, -1e30)
    crossed = jnp.where(ids[other] <= ids[own], 0.0, -1e30)
    masks = [
        jnp.where(key_swapped, 0.0, straight),
        jnp.where(key_swapped, straight, 0.0),
        jnp.where(key_swapped, crossed, 0.0),
        jnp.where(key_swapped, 0.0, crossed),
    ]
    side_ref[pl.ds(0, 6), :] = jnp.concatenate([gate(other), gate(own), *masks], axis=0)
    for fetch in fetches[:count]:
        fetch.wait()


def attend_kernel(side_ref, own_ref, other_ref, out_ref):
    members, pair, rows, _ = out_ref.shape
    group_rows = members * rows
    factor = LOG2_E / HEAD**0.5
    swapped = [place ^ FIRST in SWAPPED for place in range(members)]
    cuts = [0, *(place for place in range(1, members) if swapped[place] != swapped[place - 1]), members]
    runs = [(slice(start * rows, stop * rows), swapped[start]) for start, stop in zip(cuts, cuts[1:])]

    def tokens(ref, part, head):
        return ref[:, pl.ds((part * pair + head) * rows, rows), :].reshape(group_rows, HEAD)

    def dot(a, b, contract):
        return lax.dot_general(a, b, ((contract[:1], contract[1:]), ((), ())), preferred_element_type=jnp.float32)

    def masked(score, side):
        masks = [side_ref[2 + 2 * kind + side : 3 + 2 * kind + side, :] for kind in range(2)]
        return jnp.concatenate([score[run] + masks[kind] for run, kind in runs], axis=0)

    ones = jnp.ones((group_rows, HEAD), jnp.bfloat16)
    refs = (own_ref, other_ref)
    scores = [
        [dot(tokens(other_ref, 0, head), tokens(ref, 1, head), (1, 1)) for ref in refs] for head in range(pair)
    ]
    weights = []
    for head in range(pair):
        blocks = [masked(score, side) for side, score in enumerate(scores[head])]
        peak = jnp.max(jnp.maximum(*blocks), axis=1, keepdims=True)
        weights.append([jnp.exp2((block - peak) * factor).astype(jnp.bfloat16) for block in blocks])
    summed = []
    for head in range(pair):
        values = [jnp.concatenate([tokens(ref, 2, head), ones], axis=1) for ref in refs]
        summed.append(sum(dot(weight, value, (1, 0)) for weight, value in zip(weights[head], values)))
    for head in range(pair):
        attended = (summed[head][:, :HEAD] / summed[head][:, HEAD:]).astype(jnp.bfloat16).astype(jnp.float32)
        gates = [side_ref[kind : kind + 1, head * HEAD : (head + 1) * HEAD] for kind in range(2)]
        done = jnp.concatenate([attended[run] * gates[kind] for run, kind in runs], axis=0).astype(jnp.bfloat16)
        out_ref[:, head] = done.reshape(members, rows, HEAD)


def unpack_kernel(heads_ref, out_ref, sems):
    tiles, places = out_ref.shape[:2]
    pairs = [
        (heads_ref.at[half, :, tile], out_ref.at[tile, half]) for tile in range(tiles) for half in halves(places)
    ]
    copies = [pltpu.make_async_copy(*pair, sems.at[i]) for i, pair in enumerate(pairs)]
    for copy in copies:
        copy.start()
    for copy in copies:
        copy.wait()


def in_vmem(array):
    return pltpu.with_memory_space_constraint(array, pltpu.VMEM)


def tiled(states, members):
    rows, columns = states.shape
    pair = columns // HEAD // members
    return states.reshape(rows // TILE, TILE, members, pair, HEAD).transpose(0, 2, 3, 1, 4)


def exchanged(chunks):
    groups = teams(chunks.shape[0])
    return lax.all_to_all(chunks, ("group", "ctx"), split_axis=0, concat_axis=0, tiled=True, axis_index_groups=groups)


def local(queries, key_states, value_states, gate_table, noise_levels, group_ids):
    rows = queries.shape[0]
    tiles = rows // TILE
    members = lax.axis_size("ctx")
    pair = HEADS // members
    whole = pl.BlockSpec(memory_space=pltpu.VMEM)
    hbm = pl.BlockSpec(memory_space=pltpu.HBM)
    states = (tiled(array, members) for array in (queries, key_states, value_states))
    sources = (noise_levels, group_ids, gate_table, *states)
    packed, side = pl.pallas_call(
        pack_kernel,
        out_shape=[
            pltpu.VMEM((members, 3, pair, tiles, TILE, HEAD), jnp.bfloat16),
            pltpu.VMEM((8, members * rows), jnp.float32),
        ],
        in_specs=[hbm] * len(sources),
        out_specs=[whole, whole],
        scratch_shapes=[
            pltpu.SMEM(noise_levels.shape, jnp.int32),
            pltpu.SMEM(group_ids.shape, jnp.int32),
            pltpu.VMEM((gate_table.shape[0], pair * HEAD), jnp.float32),
            pltpu.SemaphoreType.DMA((3 + 6 * tiles,)),
        ],
    )(*(pltpu.with_memory_space_constraint(source, pltpu.HBM) for source in sources))
    own = exchanged(packed.reshape(members, 3 * pair * rows, HEAD))
    other = lax.ppermute(own, "group", [(0, 1), (1, 0)])
    done = pl.pallas_call(
        attend_kernel,
        out_shape=pltpu.VMEM((members, pair, rows, HEAD), jnp.bfloat16),
        in_specs=[whole] * 3,
        out_specs=whole,
    )(in_vmem(side), in_vmem(own), in_vmem(other))
    returned = exchanged(done.reshape(members, pair * rows, HEAD))
    handed = pl.pallas_call(
        unpack_kernel,
        out_shape=pltpu.HBM((tiles, members, pair, TILE, HEAD), jnp.bfloat16),
        in_specs=[whole],
        out_specs=hbm,
        scratch_shapes=[pltpu.SemaphoreType.DMA((2 * tiles,))],
    )(in_vmem(returned.reshape(members, pair, tiles, TILE, HEAD)))
    return handed.transpose(0, 3, 1, 2, 4).reshape(rows, HEADS * HEAD)


def shifted(block, axis, distance):
    devices = range(lax.axis_size(axis))
    route = [((i - distance) % len(devices), i) for i in devices]
    return lax.ppermute(block, axis, route)


def doubled(states):
    row_count = states.shape[0]
    shaped = states.reshape(row_count, HEADS, 1, HEAD)
    return jnp.broadcast_to(shaped, (row_count, HEADS, 2, HEAD)).reshape(row_count, 2 * HEADS, HEAD)


def attend(running, chosen, key_block, value_block, key_group, group_ids, own_id):
    peak, total, summed = running
    marked = key_group[:, None] == jnp.arange(group_ids.shape[0], dtype=jnp.int32)[None, :]
    key_ids = jnp.sum(jnp.where(marked, group_ids[None, :], 0), axis=1)
    allowed = (key_ids <= own_id)[None, None, :]
    scores = jnp.einsum("pqd,rpd->pqr", chosen, key_block, preferred_element_type=jnp.float32)
    scores = jnp.where(allowed, scores * (1.0 / HEAD**0.5), -1e30)
    new_peak = jnp.maximum(peak, jnp.max(scores, axis=-1))
    weights = jnp.where(allowed, jnp.exp(scores - new_peak[..., None]), 0.0)
    total = jnp.sum(weights, axis=-1)
    summed = jnp.einsum(
        "pqr,rpd->pqd",
        weights.astype(jnp.bfloat16),
        value_block,
        preferred_element_type=jnp.float32,
    )
    return (new_peak, total, summed)


def local_wide(queries, key_states, value_states, gate_table, noise_levels, group_ids):
    tok_count = queries.shape[0]
    ctx_count = lax.axis_size("ctx")
    group_count = lax.axis_size("group")
    slot_count = 2 * HEADS // ctx_count
    group_rows = tok_count * ctx_count
    half_rows = group_rows // 2
    section_marks = jnp.arange(group_count, dtype=jnp.int32) == lax.axis_index("group")
    own_id = jnp.sum(jnp.where(section_marks, group_ids, 0))
    own_level = jnp.sum(jnp.where(section_marks, noise_levels, 0))
    slot_index = lax.axis_index("ctx") * slot_count + jnp.arange(slot_count, dtype=jnp.int32)
    offsets = slot_index % 2 * half_rows

    def select(offset, block):
        return lax.dynamic_slice_in_dim(block, offset, half_rows, 0)

    initial = (
        jnp.full((slot_count, half_rows), -1e30, jnp.float32),
        jnp.zeros((slot_count, half_rows), jnp.float32),
        jnp.zeros((slot_count, half_rows, HEAD), jnp.float32),
    )
    query_heads, key_heads, value_heads = (
        lax.all_to_all(doubled(queries), "ctx", split_axis=1, concat_axis=0, tiled=True),
        lax.all_to_all(doubled(key_states), "ctx", split_axis=1, concat_axis=0, tiled=True),
        lax.all_to_all(doubled(value_states), "ctx", split_axis=1, concat_axis=0, tiled=True),
    )
    chosen = jax.vmap(select, in_axes=(0, 1))(offsets, query_heads)
    key_piece = lax.all_gather(key_heads, "group", axis=0, tiled=True)
    value_piece = lax.all_gather(value_heads, "group", axis=0, tiled=True)
    key_group = jnp.arange(key_piece.shape[0], dtype=jnp.int32) // group_rows
    running = attend(initial, chosen, key_piece, value_piece, key_group, group_ids, own_id)
    peak, total, summed = running
    attended = (summed / total[..., None]).astype(jnp.bfloat16)

    def place(offset, block):
        return lax.dynamic_update_slice_in_dim(
            jnp.zeros((group_rows, HEAD), jnp.bfloat16), block, offset, 0
        )

    spread = jax.vmap(place, out_axes=1)(offsets, attended)
    returned = lax.all_to_all(spread, "ctx", split_axis=0, concat_axis=1, tiled=True)
    paired = returned.reshape(tok_count, HEADS, 2, HEAD)
    merged = (paired[:, :, 0] + paired[:, :, 1]).reshape(tok_count, HEADS * HEAD)
    level_marks = jnp.arange(gate_table.shape[0], dtype=jnp.int32)[:, None] == own_level
    gate_row = jnp.sum(jnp.where(level_marks, gate_table, 0.0), axis=0)
    done = (merged.astype(jnp.float32) * gate_row[None, :]).astype(jnp.bfloat16)
    return shifted(done, "group", 1)


def solution(mesh):
    in_pairs = mesh.shape["group"] == 2 and 2 * mesh.shape["ctx"] == HEADS
    tokens = P(("group", "ctx"), None)
    return jax.shard_map(
        local if in_pairs else local_wide,
        mesh=mesh,
        in_specs=(tokens, tokens, tokens, P(), P(), P()),
        out_specs=tokens,
        check_vma=False,
    )
```

```python
import functools

import jax
import jax.numpy as jnp
from jax import lax
from jax.experimental import pallas as pl
from jax.experimental.pallas import tpu as pltpu
from jax.sharding import PartitionSpec as P

HEADS = 32
HEAD = 128
LOG2_E = 1.4426950408889634
TILE = 8
FIRST = 11
SWAPPED = (0,)


def teams(members):
    order = [place ^ FIRST for place in range(members)]
    return [[(team ^ (member in SWAPPED)) * members + member for member in order] for team in range(2)]


def own_team():
    team = lax.axis_index("group")
    for member in SWAPPED:
        team = jnp.where(lax.axis_index("ctx") == member, 1 - team, team)
    return team


def pack_kernel(
    levels_ref, ids_ref, gate_ref, query_ref, key_ref, value_ref,
    packed_ref, side_ref, levels, ids, gate_block, sems,
):
    width = gate_block.shape[1]
    place = lax.axis_index("ctx") ^ FIRST
    columns = pl.ds(pl.multiple_of(place * width, width), width)
    pairs = []
    for part, ref in enumerate((query_ref, key_ref, value_ref)):
        for tile in range(ref.shape[0]):
            pairs.append((ref.at[tile], packed_ref.at[:, part, :, tile]))
    count = len(pairs)
    pairs += [(levels_ref, levels), (ids_ref, ids), (gate_ref.at[:, columns], gate_block)]
    fetches = [pltpu.make_async_copy(*pair, sems.at[i]) for i, pair in enumerate(pairs)]
    for fetch in fetches:
        fetch.start()
    for fetch in fetches[count:]:
        fetch.wait()
    own = own_team()
    other = 1 - own
    level_rows = lax.broadcasted_iota(jnp.int32, gate_block.shape, 0)

    def gate(group):
        return jnp.sum(jnp.where(level_rows == levels[group], gate_block[...], 0.0), axis=0, keepdims=True)

    keys = side_ref.shape[1]
    key_place = lax.broadcasted_iota(jnp.int32, (1, keys), 1) // (keys // packed_ref.shape[0])
    key_swapped = functools.reduce(jnp.logical_or, [key_place == member ^ FIRST for member in SWAPPED])
    straight = jnp.where(ids[own] <= ids[other], 0.0, -1e30)
    crossed = jnp.where(ids[other] <= ids[own], 0.0, -1e30)
    masks = [
        jnp.where(key_swapped, 0.0, straight),
        jnp.where(key_swapped, straight, 0.0),
        jnp.where(key_swapped, crossed, 0.0),
        jnp.where(key_swapped, 0.0, crossed),
    ]
    side_ref[pl.ds(0, 6), :] = jnp.concatenate([gate(other), gate(own), *masks], axis=0)
    for fetch in fetches[:count]:
        fetch.wait()


def attend_kernel(side_ref, own_ref, other_ref, out_ref):
    members, pair, rows, _ = out_ref.shape
    group_rows = members * rows
    factor = LOG2_E / HEAD**0.5
    swapped = [place ^ FIRST in SWAPPED for place in range(members)]
    half = members // 2
    starts = [(head, first) for head in range(pair) for first in (0, half)]

    def runs_from(first):
        inner = [cut for cut in range(1, half) if swapped[first + cut] != swapped[first + cut - 1]]
        cuts = [0, *inner, half]
        return [(slice(i * rows, j * rows), swapped[first + i]) for i, j in zip(cuts, cuts[1:])]

    def tokens(ref, part, head):
        return ref[:, pl.ds((part * pair + head) * rows, rows), :].reshape(group_rows, HEAD)

    def dot(a, b, contract):
        return lax.dot_general(a, b, ((contract[:1], contract[1:]), ((), ())), preferred_element_type=jnp.float32)

    def masked(score, side, first):
        masks = [side_ref[2 + 2 * kind + side : 3 + 2 * kind + side, :] for kind in range(2)]
        return jnp.concatenate([score[run] + masks[kind] for run, kind in runs_from(first)], axis=0)

    ones = jnp.ones((group_rows, HEAD), jnp.bfloat16)
    refs = (own_ref, other_ref)
    queries = [tokens(other_ref, 0, head) for head in range(pair)]
    scores = [
        [dot(queries[head][first * rows : (first + half) * rows], tokens(ref, 1, head), (1, 1)) for ref in refs]
        for head, first in starts
    ]
    weights = []
    for (head, first), score in zip(starts, scores):
        blocks = [masked(block, side, first) for side, block in enumerate(score)]
        peak = jnp.max(jnp.maximum(*blocks), axis=1, keepdims=True)
        weights.append([jnp.exp2((block - peak) * factor).astype(jnp.bfloat16) for block in blocks])
    summed = []
    for (head, first), weight in zip(starts, weights):
        values = [jnp.concatenate([tokens(ref, 2, head), ones], axis=1) for ref in refs]
        summed.append(sum(dot(w, value, (1, 0)) for w, value in zip(weight, values)))
    for (head, first), total in zip(starts, summed):
        attended = (total[:, :HEAD] / total[:, HEAD:]).astype(jnp.bfloat16).astype(jnp.float32)
        gates = [side_ref[kind : kind + 1, head * HEAD : (head + 1) * HEAD] for kind in range(2)]
        done = jnp.concatenate([attended[run] * gates[kind] for run, kind in runs_from(first)], axis=0)
        out_ref[pl.ds(first, half), head] = done.astype(jnp.bfloat16).reshape(half, rows, HEAD)


def unpack_kernel(heads_ref, out_ref, sems):
    copies = [
        pltpu.make_async_copy(heads_ref.at[:, :, tile], out_ref.at[tile], sems.at[tile])
        for tile in range(out_ref.shape[0])
    ]
    for copy in copies:
        copy.start()
    for copy in copies:
        copy.wait()


def in_vmem(array):
    return pltpu.with_memory_space_constraint(array, pltpu.VMEM)


def tiled(states, members):
    rows, columns = states.shape
    pair = columns // HEAD // members
    return states.reshape(rows // TILE, TILE, members, pair, HEAD).transpose(0, 2, 3, 1, 4)


def exchanged(chunks):
    groups = teams(chunks.shape[0])
    return lax.all_to_all(chunks, ("group", "ctx"), split_axis=0, concat_axis=0, tiled=True, axis_index_groups=groups)


def local(queries, key_states, value_states, gate_table, noise_levels, group_ids):
    rows = queries.shape[0]
    tiles = rows // TILE
    members = lax.axis_size("ctx")
    pair = HEADS // members
    whole = pl.BlockSpec(memory_space=pltpu.VMEM)
    hbm = pl.BlockSpec(memory_space=pltpu.HBM)
    states = (tiled(array, members) for array in (queries, key_states, value_states))
    sources = (noise_levels, group_ids, gate_table, *states)
    packed, side = pl.pallas_call(
        pack_kernel,
        out_shape=[
            pltpu.VMEM((members, 3, pair, tiles, TILE, HEAD), jnp.bfloat16),
            pltpu.VMEM((8, members * rows), jnp.float32),
        ],
        in_specs=[hbm] * len(sources),
        out_specs=[whole, whole],
        scratch_shapes=[
            pltpu.SMEM(noise_levels.shape, jnp.int32),
            pltpu.SMEM(group_ids.shape, jnp.int32),
            pltpu.VMEM((gate_table.shape[0], pair * HEAD), jnp.float32),
            pltpu.SemaphoreType.DMA((3 + 3 * tiles,)),
        ],
    )(*(pltpu.with_memory_space_constraint(source, pltpu.HBM) for source in sources))
    own = exchanged(packed.reshape(members, 3 * pair * rows, HEAD))
    other = lax.ppermute(own, "group", [(0, 1), (1, 0)])
    done = pl.pallas_call(
        attend_kernel,
        out_shape=pltpu.VMEM((members, pair, rows, HEAD), jnp.bfloat16),
        in_specs=[whole] * 3,
        out_specs=whole,
    )(in_vmem(side), in_vmem(own), in_vmem(other))
    returned = exchanged(done.reshape(members, pair * rows, HEAD))
    handed = pl.pallas_call(
        unpack_kernel,
        out_shape=pltpu.HBM((tiles, members, pair, TILE, HEAD), jnp.bfloat16),
        in_specs=[whole],
        out_specs=hbm,
        scratch_shapes=[pltpu.SemaphoreType.DMA((tiles,))],
    )(in_vmem(returned.reshape(members, pair, tiles, TILE, HEAD)))
    return handed.transpose(0, 3, 1, 2, 4).reshape(rows, HEADS * HEAD)


def shifted(block, axis, distance):
    devices = range(lax.axis_size(axis))
    route = [((i - distance) % len(devices), i) for i in devices]
    return lax.ppermute(block, axis, route)


def doubled(states):
    row_count = states.shape[0]
    shaped = states.reshape(row_count, HEADS, 1, HEAD)
    return jnp.broadcast_to(shaped, (row_count, HEADS, 2, HEAD)).reshape(row_count, 2 * HEADS, HEAD)


def attend(running, chosen, key_block, value_block, key_group, group_ids, own_id):
    peak, total, summed = running
    marked = key_group[:, None] == jnp.arange(group_ids.shape[0], dtype=jnp.int32)[None, :]
    key_ids = jnp.sum(jnp.where(marked, group_ids[None, :], 0), axis=1)
    allowed = (key_ids <= own_id)[None, None, :]
    scores = jnp.einsum("pqd,rpd->pqr", chosen, key_block, preferred_element_type=jnp.float32)
    scores = jnp.where(allowed, scores * (1.0 / HEAD**0.5), -1e30)
    new_peak = jnp.maximum(peak, jnp.max(scores, axis=-1))
    weights = jnp.where(allowed, jnp.exp(scores - new_peak[..., None]), 0.0)
    total = jnp.sum(weights, axis=-1)
    summed = jnp.einsum(
        "pqr,rpd->pqd",
        weights.astype(jnp.bfloat16),
        value_block,
        preferred_element_type=jnp.float32,
    )
    return (new_peak, total, summed)


def local_wide(queries, key_states, value_states, gate_table, noise_levels, group_ids):
    tok_count = queries.shape[0]
    ctx_count = lax.axis_size("ctx")
    group_count = lax.axis_size("group")
    slot_count = 2 * HEADS // ctx_count
    group_rows = tok_count * ctx_count
    half_rows = group_rows // 2
    section_marks = jnp.arange(group_count, dtype=jnp.int32) == lax.axis_index("group")
    own_id = jnp.sum(jnp.where(section_marks, group_ids, 0))
    own_level = jnp.sum(jnp.where(section_marks, noise_levels, 0))
    slot_index = lax.axis_index("ctx") * slot_count + jnp.arange(slot_count, dtype=jnp.int32)
    offsets = slot_index % 2 * half_rows

    def select(offset, block):
        return lax.dynamic_slice_in_dim(block, offset, half_rows, 0)

    initial = (
        jnp.full((slot_count, half_rows), -1e30, jnp.float32),
        jnp.zeros((slot_count, half_rows), jnp.float32),
        jnp.zeros((slot_count, half_rows, HEAD), jnp.float32),
    )
    query_heads, key_heads, value_heads = (
        lax.all_to_all(doubled(queries), "ctx", split_axis=1, concat_axis=0, tiled=True),
        lax.all_to_all(doubled(key_states), "ctx", split_axis=1, concat_axis=0, tiled=True),
        lax.all_to_all(doubled(value_states), "ctx", split_axis=1, concat_axis=0, tiled=True),
    )
    chosen = jax.vmap(select, in_axes=(0, 1))(offsets, query_heads)
    key_piece = lax.all_gather(key_heads, "group", axis=0, tiled=True)
    value_piece = lax.all_gather(value_heads, "group", axis=0, tiled=True)
    key_group = jnp.arange(key_piece.shape[0], dtype=jnp.int32) // group_rows
    running = attend(initial, chosen, key_piece, value_piece, key_group, group_ids, own_id)
    peak, total, summed = running
    attended = (summed / total[..., None]).astype(jnp.bfloat16)

    def place(offset, block):
        return lax.dynamic_update_slice_in_dim(
            jnp.zeros((group_rows, HEAD), jnp.bfloat16), block, offset, 0
        )

    spread = jax.vmap(place, out_axes=1)(offsets, attended)
    returned = lax.all_to_all(spread, "ctx", split_axis=0, concat_axis=1, tiled=True)
    paired = returned.reshape(tok_count, HEADS, 2, HEAD)
    merged = (paired[:, :, 0] + paired[:, :, 1]).reshape(tok_count, HEADS * HEAD)
    level_marks = jnp.arange(gate_table.shape[0], dtype=jnp.int32)[:, None] == own_level
    gate_row = jnp.sum(jnp.where(level_marks, gate_table, 0.0), axis=0)
    done = (merged.astype(jnp.float32) * gate_row[None, :]).astype(jnp.bfloat16)
    return shifted(done, "group", 1)


def solution(mesh):
    in_pairs = mesh.shape["group"] == 2 and 2 * mesh.shape["ctx"] == HEADS
    tokens = P(("group", "ctx"), None)
    return jax.shard_map(
        local if in_pairs else local_wide,
        mesh=mesh,
        in_specs=(tokens, tokens, tokens, P(), P(), P()),
        out_specs=tokens,
        check_vma=False,
    )
```
